32 devices in a mesh: expert: 4 (over y, core), dp: 8 (over z, x).
Axes of the slice: x: 2, y: 2, z: 4, core: 2. Of those that a mesh axis runs over, the one named last changes fastest.
Arguments:
- tokens: bfloat16 [4096, 3584], P(('expert', 'dp')), may hold values from -6 to 6
- grad_out: bfloat16 [4096, 3584], P(('expert', 'dp')), may hold values from -4 to 4
- route_weights: float32 [4096, 8], P(('expert', 'dp')), may hold values from 0.05 to 0.5
- expert_ids: int32 [4096, 8], P(('expert', 'dp')), may hold values from 0 to 255, all different within a row; in each aligned block of 128 rows (0 to 127, 128 to 255, ...) at most 5 rows name the same one
- swap_code: int32 [4], replicated, may hold values from 0 to 3, as said below
- w_in: bfloat16 [4, 2, 2048, 3584], P('expert', None, 'dp'), may hold values from -0.09375 to 0.09375
- w_down: bfloat16 [4, 2048, 3584], P('expert', 'dp'), may hold values from -0.125 to 0.125
- moment1: float32 [4, 2048, 3584], P('expert', 'dp'), may hold values from -6 to 6
- moment2: float32 [4, 2048, 3584], P('expert', 'dp'), may hold values from 0.05 to 1
Outputs:
- new_down: bfloat16 [4, 2048, 3584], P('expert', 'dp')
- new_moment1: float32 [4, 2048, 3584], P('expert', 'dp')
- new_moment2: float32 [4, 2048, 3584], P('expert', 'dp')
- grad_in: bfloat16 [4, 2, 2048, 3584], P('expert', None, 'dp')
The draws below stay inside these ranges and needn't reach their ends.
Inputs may be any that keep to these rules, and one draw needn't show every extreme that they name: `expert_ids`: each row names 8 different experts; in the rows of one device no expert is named more than 5 times. `swap_code`: entry 0 has all of its 2 low bits set.
All inputs are finite; a program needn't handle non-finite values.
Results may differ from the reference program's by a relative error of at most 0.0057.
Values may be sent and summed in bfloat16 or wider, within the bound.
No kernel may reach another device: no remote copies, remote signals or barrier semaphores. Data moves between devices by JAX's collectives and lax.ppermute only.
A program may use at most 128 MiB of HBM per device.

```python
import math
import jax
import jax.numpy as jnp
import numpy as np
from jax import lax

D = 3584
FF = 2048
E_ALL = 256
TOP = 8
TOK_DEV = 128
CAP = 5
EXPERTS = 4
SECTIONS = 2
TOKENS = 4096


def draw_swap_code(key, part):
    codes = jax.random.randint(key, (EXPERTS,), 0, EXPERTS, dtype=jnp.int32)
    return codes.at[0].set(EXPERTS - 1)


def level_of(own_key, extent, shards, least, largest):
    def one(dim, shards_of):
        draws = jax.random.uniform(jax.random.fold_in(jax.random.fold_in(own_key, 6), dim), (shards_of,), jnp.float32, least / len(shards), largest / len(shards))
        return jnp.repeat(jnp.exp(draws), extent[dim] // shards_of).reshape((-1,) + (1,) * (len(extent) - dim - 1))

    loudness = one(*shards[0])
    for cut in shards[1:]:
        loudness = loudness * one(*cut)
    return loudness


def shared_out(own_key, own, number, rows, number_of, top, bound, slope):
    ranking = jax.random.permutation(own_key, number_of)
    heavy_load, ordinary = shares(number_of, rows * top, bound, slope, True), shares(number_of, rows * top, bound, slope, False)
    places = jnp.arange(number_of)

    def named(tallies, offset_by):
        used = int((tallies > 0).sum())
        fixed = max(1, used // 4)
        moved = fixed + (places - fixed + offset_by * (used - fixed)) % max(1, number_of - fixed)
        return jnp.zeros((number_of,), jnp.int32).at[ranking[jnp.where(places < fixed, places, moved)]].set(jnp.asarray(tallies, jnp.int32))

    tallies = jnp.where(number % 4 == 0, named(heavy_load, number // 4), named(ordinary, number - number // 4 - 1))
    mixed = jax.random.permutation(jax.random.fold_in(own, 3), number_of)
    source_of, receiver = mixed[0:number_of // 2 * 2:2], mixed[1:number_of // 2 * 2:2]
    room = jnp.minimum(tallies[source_of] - 1, bound - tallies[receiver]) // 2
    room = jnp.where((source_of == ranking[0]) | (receiver == ranking[0]) | (tallies[receiver] == 0), 0, jnp.maximum(room, 0))
    moved = jax.random.randint(jax.random.fold_in(own, 4), (number_of // 2,), 0, 1 << 20) % (room + 1)
    tallies = tallies.at[source_of].add(-moved).at[receiver].add(moved)
    members = jnp.searchsorted(jnp.cumsum(tallies), jnp.arange(rows * top), side="right").astype(jnp.int32)
    listing = members.reshape(top, rows).T
    listing = listing[jax.random.permutation(jax.random.fold_in(own, 1), rows)]
    offset_by = jax.random.randint(jax.random.fold_in(own, 2), (rows, 1), 0, top)
    return jnp.take_along_axis(listing, (jnp.arange(top)[None, :] + offset_by) % top, axis=1)


def shares(amount, total, limit, skew, full):
    loads = [(1 << 20) // math.isqrt(rank ** skew) + 1 for rank in range(1, amount + 1)]
    largest = limit if full else min(limit, max(-(-total // amount), total * loads[0] // sum(loads)))
    least = 1 if total - largest >= amount - 1 else 0
    counts, rest = [largest] + [least] * (amount - 1), total - largest - least * (amount - 1)
    while rest > 0:
        candidates = [i for i in range(1, amount) if counts[i] < largest] or [i for i in range(1, amount) if counts[i] < limit]
        pool, left = sum([loads[i] for i in candidates]), rest
        for i in candidates:
            extra = min(limit - counts[i], max(1, left * loads[i] // pool), rest)
            counts[i] = counts[i] + extra
            rest = rest - extra
    return np.array(counts)


def noise(own_key, extent, scale, reach, shards=(), kind=jnp.bfloat16):
    loudness = level_of(own_key, extent, shards, -0.22, 0.18) if shards else 1.0
    result = jax.random.normal(own_key, extent, jnp.float32) * scale * loudness
    return jnp.minimum(jnp.maximum(result, -reach), reach).astype(kind)


def setup_inputs(seed: int = 0) -> dict:
    key_list = jax.random.split(jax.random.key(seed), 10)
    tokens = noise(key_list[0], (TOKENS, D), 1.0, 6.0, ((0, 32),))
    grad_out = noise(key_list[1], (TOKENS, D), 0.3, 4.0, ((0, 32),))
    route_weights = jnp.clip(jnp.exp(math.log(0.5) - 2.3025851 * jax.random.uniform(key_list[2], (TOKENS, TOP), jnp.float32) ** level_of(key_list[2], (TOKENS, TOP), ((0, 32),), -0.2, 0.2)), 0.05, 0.5)
    expert_ids_keys = jax.random.split(jax.random.fold_in(key_list[3], 1), TOKENS // TOK_DEV)
    expert_ids_turns = jax.random.permutation(jax.random.fold_in(key_list[3], 3), TOKENS // TOK_DEV)
    expert_ids = jax.vmap(lambda own, number: shared_out(jax.random.fold_in(key_list[3], 2), own, number, TOK_DEV, E_ALL, TOP, CAP, 1))(expert_ids_keys, expert_ids_turns).reshape((TOKENS, TOP))
    swap_code = draw_swap_code(jax.random.fold_in(key_list[9], 71), 0)
    w_in = noise(key_list[5], (EXPERTS, 2, FF, D), D ** -0.5, 0.09375, ((0, 4), (2, 8)))
    w_down = noise(key_list[6], (EXPERTS, FF, D), FF ** -0.5, 0.125, ((0, 4), (1, 8)))
    moment1 = noise(key_list[7], (EXPERTS, FF, D), 1.0, 6.0, ((0, 4), (1, 8)), jnp.float32)
    moment2 = jnp.clip(jnp.exp(math.log(1.0) - 2.9957323 * jax.random.uniform(key_list[8], (EXPERTS, FF, D), jnp.float32) ** level_of(key_list[8], (EXPERTS, FF, D), ((0, 4), (1, 8)), -0.2, 0.2)), 0.05, 1.0)
    return dict(tokens=tokens, grad_out=grad_out, route_weights=route_weights, expert_ids=expert_ids, swap_code=swap_code, w_in=w_in, w_down=w_down, moment1=moment1, moment2=moment2)


adam_rate = 0.01
beta_one = 0.9
beta_two = 0.999
adam_step = 100.0
adam_eps = 1e-08

def contract(left_side, right_side, left_dim, right_dim):
    return lax.dot_general(left_side, right_side, (((left_dim,), (right_dim,)), ((), ())), preferred_element_type=jnp.float32)

def forward_rows(token_rows, w_gate, w_up):
    gate_proj = contract(token_rows, w_gate, 1, 1)
    up_proj = contract(token_rows, w_up, 1, 1)
    sigmoid_val = jax.nn.sigmoid(gate_proj)
    activated = gate_proj * sigmoid_val
    slopes = sigmoid_val * (1.0 + gate_proj * (1.0 - sigmoid_val))
    hidden = (activated * up_proj).astype(jnp.bfloat16)
    return (up_proj, activated, slopes, hidden)

def backward_rows(token_rows, grad_rows, up_proj, activated, slopes, hidden, w_dn):
    back_grad = contract(grad_rows, w_dn, 1, 1)
    gate_back = (back_grad * up_proj * slopes).astype(jnp.bfloat16)
    up_back = (back_grad * activated).astype(jnp.bfloat16)
    return (contract(hidden, grad_rows, 0, 0), contract(gate_back, token_rows, 0, 0), contract(up_back, token_rows, 0, 0))

def slot_order(swap_code):
    slot_ids = jnp.arange(EXPERTS, dtype=jnp.int32)
    source = slot_ids
    for section_bit in range(SECTIONS):
        partner_slot = jnp.bitwise_xor(slot_ids, 1 << section_bit)
        lower_slot = jnp.minimum(slot_ids, partner_slot)
        swapped = swap_code[lower_slot] // (1 << section_bit) % 2 == 1
        source = source[jnp.where(swapped, partner_slot, slot_ids)]
    return source

def reference(tokens, grad_out, route_weights, expert_ids, swap_code, w_in, w_down, moment1, moment2):
    most_rows = CAP * (TOKENS // TOK_DEV)
    row_ids = jnp.arange(most_rows, dtype=jnp.int32)

    def one_expert(packed):
        expert, weight_in, weight_down = packed
        hits = expert_ids == expert
        picked = jnp.any(hits, axis=1)
        row_scale = lax.optimization_barrier(jnp.sum(jnp.where(hits, route_weights, 0.0), axis=1))
        chosen = jnp.nonzero(picked, size=most_rows, fill_value=0)[0].astype(jnp.int32)
        filled = row_ids < jnp.sum(picked.astype(jnp.int32))
        token_rows = jnp.where(filled[:, None], tokens[chosen], jnp.zeros((), tokens.dtype))
        weights_used = jnp.where(filled, row_scale[chosen], 0.0)
        grad_rows = (grad_out[chosen].astype(jnp.float32) * weights_used[:, None]).astype(jnp.bfloat16)
        up_proj, activated, slopes, hidden = forward_rows(token_rows, weight_in[0], weight_in[1])
        down_grad, gate_grad, up_grad = backward_rows(token_rows, grad_rows, up_proj, activated, slopes, hidden, weight_down)
        return (down_grad, jnp.stack([gate_grad, up_grad]))
    down_grad, in_grad = lax.map(one_expert, (jnp.arange(EXPERTS, dtype=jnp.int32), w_in, w_down))
    first_new = beta_one * moment1 + (1.0 - beta_one) * down_grad
    second_new = beta_two * moment2 + (1.0 - beta_two) * down_grad * down_grad
    fix_one = 1.0 - beta_one ** adam_step
    fix_two = 1.0 - beta_two ** adam_step
    step_size = first_new / fix_one / (jnp.sqrt(second_new / fix_two) + adam_eps)
    updated = (w_down.astype(jnp.float32) - adam_rate * step_size).astype(jnp.bfloat16)
    source = slot_order(swap_code)
    return (updated[source], first_new[source], second_new[source], in_grad.astype(jnp.bfloat16)[source])
```

```python
import functools
import itertools

import jax
import jax.numpy as jnp
from jax import lax
from jax.experimental import pallas as pl
from jax.experimental.pallas import tpu as pltpu
from jax.sharding import PartitionSpec as P

CAP = 5
VMEM_LIMIT = 40 * 1024 * 1024

adam_rate = 0.01
beta_one = 0.9
beta_two = 0.999
adam_step = 100.0
adam_eps = 1e-08


def dot(left_side, right_side, left_dim, right_dim):
    return lax.dot_general(
        left_side,
        right_side,
        (((left_dim,), (right_dim,)), ((), ())),
        preferred_element_type=jnp.float32,
    )


def params():
    return pltpu.CompilerParams(vmem_limit_bytes=VMEM_LIMIT)


def cost(flops, nbytes):
    return pl.CostEstimate(flops=int(flops), bytes_accessed=int(nbytes), transcendentals=0)


def tile_of(width, most):
    tile = 128
    for count in range(1, width // 128 + 1):
        if width % (count * 128) == 0 and count * 128 <= most:
            tile = count * 128
    return tile


def pick_kernel(expert_count, ids_ref, weights_ref, tok_ref, grad_ref, out_ref, sel_t, sel_g, scale):
    rows = tok_ref.shape[0]
    half = expert_count * CAP

    @pl.when(pl.program_id(0) == 0)
    def _():
        ids = ids_ref[...]
        weights = weights_ref[...]
        earlier = (
            lax.broadcasted_iota(jnp.int32, (rows, rows), 0)
            < lax.broadcasted_iota(jnp.int32, (rows, rows), 1)
        ).astype(jnp.bfloat16)
        row = lax.broadcasted_iota(jnp.int32, (2 * half, rows), 0)
        in_half = jnp.where(row >= half, row - half, row)
        chosen = jnp.zeros((2 * half, rows), jnp.float32)
        weight = jnp.zeros((2 * half, rows), jnp.float32)
        for expert in range(expert_count):
            named = ids == expert
            hit = jnp.max(jnp.where(named, 1.0, 0.0), axis=0, keepdims=True)
            amount = jnp.sum(jnp.where(named, weights, 0.0), axis=0, keepdims=True)
            hits = jnp.broadcast_to(hit, (8, rows))
            rank = dot(hits.astype(jnp.bfloat16), earlier, 1, 0)[0:1].astype(jnp.int32)
            of_expert = jnp.logical_and(in_half >= expert * CAP, in_half < (expert + 1) * CAP)
            match = jnp.logical_and(of_expert, in_half - expert * CAP == rank)
            chosen = chosen + jnp.where(match, hit, 0.0)
            weight = weight + jnp.where(match, hit * amount, 0.0)
        is_token = row < half
        sel_t[...] = jnp.where(is_token, chosen, 0.0).astype(jnp.bfloat16)
        sel_g[...] = jnp.where(is_token, 0.0, chosen).astype(jnp.bfloat16)
        scale[...] = jnp.sum(weight, axis=1, keepdims=True)

    picked = dot(sel_t[...], tok_ref[...], 1, 0) + scale[...] * dot(sel_g[...], grad_ref[...], 1, 0)
    out_ref[...] = picked.astype(jnp.bfloat16)


def pick_rows(tokens, grad_out, route_weights, expert_ids, expert_count):
    rows, width = tokens.shape
    top = expert_ids.shape[1]
    total = 2 * expert_count * CAP
    tile = tile_of(width, 1792)
    return pl.pallas_call(
        functools.partial(pick_kernel, expert_count),
        grid=(width // tile,),
        in_specs=[
            pl.BlockSpec((top, rows), lambda j: (0, 0)),
            pl.BlockSpec((top, rows), lambda j: (0, 0)),
            pl.BlockSpec((rows, tile), lambda j: (0, j)),
            pl.BlockSpec((rows, tile), lambda j: (0, j)),
        ],
        out_specs=pl.BlockSpec((total, tile), lambda j: (0, j)),
        out_shape=jax.ShapeDtypeStruct((total, width), jnp.bfloat16),
        scratch_shapes=[
            pltpu.VMEM((total, rows), jnp.bfloat16),
            pltpu.VMEM((total, rows), jnp.bfloat16),
            pltpu.VMEM((total, 1), jnp.float32),
        ],
        compiler_params=params(),
        cost_estimate=cost(4 * total * rows * width, 4 * rows * width),
        name="pick_rows",
    )(expert_ids.T, route_weights.T, tokens, grad_out)


def factor_kernel(half, x_ref, w_in_ref, w_down_ref, out_ref, acc):
    step = pl.program_id(0)
    count, units = acc.shape[0], w_down_ref.shape[1]

    @pl.when(step == 0)
    def _():
        acc[...] = jnp.zeros_like(acc)

    x = x_ref[...]
    acc[:, 0:units] += dot(x, w_in_ref[0, 0], 1, 1)
    acc[:, units : 2 * units] += dot(x, w_in_ref[0, 1], 1, 1)
    acc[:, 2 * units : 3 * units] += dot(x, w_down_ref[0], 1, 1)

    @pl.when(step == pl.num_programs(0) - 1)
    def _():
        gate = acc[:, 0:units]
        up = acc[:, units : 2 * units]
        back = pltpu.roll(acc[:, 2 * units : 3 * units], count - half, 0)
        sig = jax.nn.sigmoid(gate)
        activated = gate * sig
        slopes = sig * (1.0 + gate * (1.0 - sig))
        hidden = pltpu.roll(activated * up, half, 0)
        is_token = lax.broadcasted_iota(jnp.int32, (count, units), 0) % (2 * half) < half
        out_ref[:, 0:units] = jnp.where(is_token, back * up * slopes, hidden).astype(jnp.bfloat16)
        out_ref[:, units : 2 * units] = jnp.where(is_token, back * activated, 0.0).astype(jnp.bfloat16)


def factors_of(x, w_in, w_down, half):
    count, width = x.shape
    units = w_down.shape[1]
    tile = tile_of(width, 896)
    return pl.pallas_call(
        functools.partial(factor_kernel, half),
        grid=(width // tile,),
        in_specs=[
            pl.BlockSpec((count, tile), lambda j: (0, j)),
            pl.BlockSpec((1, 2, units, tile), lambda j: (0, 0, 0, j)),
            pl.BlockSpec((1, units, tile), lambda j: (0, 0, j)),
        ],
        out_specs=pl.BlockSpec((count, 2 * units), lambda j: (0, 0)),
        out_shape=jax.ShapeDtypeStruct((count, 2 * units), jnp.bfloat16),
        scratch_shapes=[pltpu.VMEM((count, 3 * units), jnp.float32)],
        compiler_params=params(),
        cost_estimate=cost(6 * count * units * width, 6 * units * width + 2 * count * width),
        name="factors",
    )(x, w_in, w_down)


def grad_kernel(half, factor_ref, x_ref, out_ref):
    count, units = factor_ref.shape[0], out_ref.shape[2]
    is_token = lax.broadcasted_iota(jnp.int32, (count, units), 0) % (2 * half) < half
    both = factor_ref[:, 0:units]
    gate_back = jnp.where(is_token, both, jnp.zeros_like(both))
    x = x_ref[...]
    out_ref[0, 0] = dot(gate_back, x, 0, 0).astype(jnp.bfloat16)
    out_ref[0, 1] = dot(factor_ref[:, units : 2 * units], x, 0, 0).astype(jnp.bfloat16)


def grads_of(factors, x, half):
    count, width = x.shape
    units = factors.shape[1] // 2
    tile = tile_of(width, 896)
    return pl.pallas_call(
        functools.partial(grad_kernel, half),
        grid=(width // tile,),
        in_specs=[
            pl.BlockSpec((count, 2 * units), lambda j: (0, 0)),
            pl.BlockSpec((count, tile), lambda j: (0, j)),
        ],
        out_specs=pl.BlockSpec((1, 2, units, tile), lambda j: (0, 0, 0, j)),
        out_shape=jax.ShapeDtypeStruct((1, 2, units, width), jnp.bfloat16),
        compiler_params=params(),
        cost_estimate=cost(4 * count * units * width, 4 * units * width + 2 * count * width),
        name="in_grads",
    )(factors, x)


def pack_kernel(w_ref, one_ref, two_ref, out_ref):
    out_ref[0] = w_ref[0]
    out_ref[1] = one_ref[0].astype(jnp.bfloat16)
    out_ref[2] = two_ref[0].astype(jnp.bfloat16)


def pack(w_down, moment1, moment2, chunk, chunks):
    _, units, width = w_down.shape
    rows = units // chunks
    tile = tile_of(width, 1792)
    spec = pl.BlockSpec((1, rows, tile), lambda j: (0, chunk, j))
    return pl.pallas_call(
        pack_kernel,
        grid=(width // tile,),
        in_specs=[spec, spec, spec],
        out_specs=pl.BlockSpec((3, rows, tile), lambda j: (0, 0, j)),
        out_shape=jax.ShapeDtypeStruct((3, rows, width), jnp.bfloat16),
        compiler_params=params(),
        cost_estimate=cost(2 * rows * width, 16 * rows * width),
        name=f"pack_state_{chunk}",
    )(w_down, moment1, moment2)


def adam_kernel(half, chunk, factor_ref, x_ref, state_ref, *refs):
    down_ref, one_ref, two_ref = refs[-3:]
    count, rows = x_ref.shape[0], state_ref.shape[1]
    is_token = lax.broadcasted_iota(jnp.int32, (count, rows), 0) % (2 * half) < half
    both = factor_ref[:, chunk * rows : (chunk + 1) * rows]
    hidden = jnp.where(is_token, jnp.zeros_like(both), both)
    down_grad = dot(hidden, x_ref[...], 0, 0)
    first_new = beta_one * state_ref[1].astype(jnp.float32) + (1.0 - beta_one) * down_grad
    second_new = beta_two * state_ref[2].astype(jnp.float32) + (1.0 - beta_two) * (down_grad * down_grad)
    fix_one = 1.0 - beta_one**adam_step
    fix_two = 1.0 - beta_two**adam_step
    step_size = first_new / fix_one / (jnp.sqrt(second_new / fix_two) + adam_eps)
    down_ref[0] = (state_ref[0].astype(jnp.float32) - adam_rate * step_size).astype(jnp.bfloat16)
    one_ref[0] = first_new
    two_ref[0] = second_new


def adam_rows(factors, x, state, chunk, chunks, half, before):
    count, width = x.shape
    units = factors.shape[1] // 2
    rows = units // chunks
    tile = tile_of(width, 896)
    spec = pl.BlockSpec((1, rows, tile), lambda j: (0, chunk, j))
    shapes = tuple(
        jax.ShapeDtypeStruct((1, units, width), kind) for kind in (jnp.bfloat16, jnp.float32, jnp.float32)
    )
    return pl.pallas_call(
        functools.partial(adam_kernel, half, chunk),
        grid=(width // tile,),
        in_specs=[
            pl.BlockSpec((count, 2 * units), lambda j: (0, 0)),
            pl.BlockSpec((count, tile), lambda j: (0, j)),
            pl.BlockSpec((3, rows, tile), lambda j: (0, 0, j)),
        ]
        + [pl.BlockSpec(memory_space=pl.ANY)] * len(before),
        out_specs=[spec, spec, spec],
        out_shape=shapes,
        input_output_aliases={3 + i: i for i in range(len(before))},
        compiler_params=params(),
        cost_estimate=cost(2 * count * rows * width, 16 * rows * width + 2 * count * width),
        name=f"adam_rows_{chunk}",
    )(factors, x, state, *before)


def shifted(array, axis_sizes, which, amount):
    planes, columns = axis_sizes
    pairs = []
    for plane, column in itertools.product(range(planes), range(columns)):
        if which == 0:
            target = (plane + amount) % planes * columns + column
        else:
            target = plane * columns + (column + amount) % columns
        pairs.append((plane * columns + column, target))
    return lax.ppermute(array, "dp", pairs)


def gather_dp(block, axis_sizes):
    planes, columns = axis_sizes
    parts = [block] + [shifted(block, axis_sizes, 0, k) for k in range(1, planes)]
    parts = parts + [shifted(p, axis_sizes, 1, k) for k in range(1, columns) for p in parts]
    return jnp.concatenate(parts, axis=0)


def role_block(pieces, masks, experts, own_slot, expert_count):
    half = expert_count * CAP
    total = 2 * half
    row = jnp.arange(total, dtype=jnp.int32)
    is_grad = row // half
    contributor = row % half // CAP
    place = jnp.zeros_like(row)
    for number, mask in enumerate(masks):
        place = jnp.where(contributor == jnp.bitwise_xor(own_slot, mask), number, place)
    column = jnp.arange(len(masks) * total, dtype=jnp.int32)
    blocks = []
    for expert in experts:
        wanted = place * total + is_grad * half + expert * CAP + row % CAP
        chosen = (wanted[:, None] == column[None, :]).astype(jnp.bfloat16)
        blocks.append(dot(chosen, pieces, 1, 0).astype(jnp.bfloat16))
    return blocks


def section_swaps(swap_code, slot, sections):
    swaps = []
    for bit in range(sections):
        lower = jnp.minimum(slot, jnp.bitwise_xor(slot, 1 << bit))
        swaps.append(swap_code[lower] // (1 << bit) % 2 == 1)
    return swaps


def static_order(expert_count, sections, swapped_pairs):
    order = list(range(expert_count))
    for bit in range(sections):
        step = [s ^ (1 << bit) if (bit, min(s, s ^ (1 << bit))) in swapped_pairs else s for s in range(expert_count)]
        order = [order[s] for s in step]
    return order


def exchange(picked, sections):
    pieces, masks = [picked], [0]
    for bit in reversed(range(sections)):
        pairs = [(i, i ^ (1 << bit)) for i in range(1 << sections)]
        theirs = lax.ppermute(jnp.concatenate(pieces, axis=0), "expert", pairs)
        size = picked.shape[0]
        pieces = pieces + [theirs[i * size : (i + 1) * size] for i in range(len(pieces))]
        masks = masks + [m ^ (1 << bit) for m in masks]
    return jnp.concatenate(pieces, axis=0), masks


def layer(move, axis_sizes, sections, chunks, picked, source, w_in, w_down, moment1, moment2):
    expert_count = 1 << sections
    half = expert_count * CAP
    own_slot = lax.axis_index("expert")
    states = [move(pack(w_down, moment1, moment2, c, chunks)) for c in range(chunks)]
    pieces, masks = exchange(picked, sections)
    own_block, new_block = role_block(pieces, masks, (own_slot, source), own_slot, expert_count)
    own_rows = gather_dp(own_block, axis_sizes)
    factors = factors_of(own_rows, w_in, w_down, half)
    new_rows = gather_dp(new_block, axis_sizes)
    factors = move(factors)
    grads = grads_of(factors, new_rows, half)
    outputs = ()
    for c in range(chunks):
        outputs = adam_rows(factors, new_rows, states[c], c, chunks, half, outputs)
    return (*outputs, grads)


def local(tokens, grad_out, route_weights, expert_ids, swap_code, w_in, w_down, moment1, moment2):
    expert_count = lax.axis_size("expert")
    sections = expert_count.bit_length() - 1
    columns = max(1, expert_count // 2)
    axis_sizes = (lax.axis_size("dp") // columns, columns)
    chunks = 4
    own_slot = lax.axis_index("expert")
    picked = pick_rows(tokens, grad_out, route_weights, expert_ids, expert_count)

    slots = jnp.arange(expert_count, dtype=jnp.int32)
    order = slots
    for bit in range(sections):
        partner = jnp.bitwise_xor(slots, 1 << bit)
        swapped = swap_code[jnp.minimum(slots, partner)] // (1 << bit) % 2 == 1
        order = order[jnp.where(swapped, partner, slots)]
    source = jnp.sum(jnp.where(slots == own_slot, order, 0))
    operands = (picked, source, w_in, w_down, moment1, moment2)

    free = [(b, s) for b in range(sections) for s in range(1, expert_count) if not s >> b & 1]
    fixed = [(b, 0) for b in range(sections)]
    if len(free) <= 2:
        branches = []
        for taken in itertools.product((False, True), repeat=len(free)):
            pairs = fixed + [pair for pair, yes in zip(free, taken) if yes]
            order_now = static_order(expert_count, sections, pairs)
            move = functools.partial(
                lax.ppermute, axis_name="expert", perm=[(order_now[s], s) for s in range(expert_count)]
            )
            branches.append(functools.partial(layer, move, axis_sizes, sections, chunks))
        which = jnp.int32(0)
        for bit, slot in free:
            which = which * 2 + swap_code[slot] // (1 << bit) % 2
        return lax.switch(which, branches, *operands)

    swaps = section_swaps(swap_code, own_slot, sections)

    def move_by_sections(array):
        for bit in range(sections):
            pairs = [(i, i ^ (1 << bit)) for i in range(expert_count)]
            array = jnp.where(swaps[bit], lax.ppermute(array, "expert", pairs), array)
        return array

    return layer(move_by_sections, axis_sizes, sections, chunks, *operands)


def solution(mesh):
    placed = (
        P(("expert", "dp"), None),
        P(("expert", "dp"), None),
        P(("expert", "dp"), None),
        P(("expert", "dp"), None),
        P(),
        P("expert", None, "dp", None),
        P("expert", "dp", None),
        P("expert", "dp", None),
        P("expert", "dp", None),
    )
    return jax.shard_map(
        local,
        mesh=mesh,
        in_specs=placed,
        out_specs=(
            P("expert", "dp", None),
            P("expert", "dp", None),
            P("expert", "dp", None),
            P("expert", None, "dp", None),
        ),
        check_vma=False,
    )
```

```python
import functools
import itertools

import jax
import jax.numpy as jnp
from jax import lax
from jax.experimental import pallas as pl
from jax.experimental.pallas import tpu as pltpu
from jax.sharding import PartitionSpec as P

CAP = 5
PIECE = 24
VMEM_LIMIT = 60 * 1024 * 1024

adam_rate = 0.01
beta_one = 0.9
beta_two = 0.999
adam_step = 100.0
adam_eps = 1e-08


def dot(left_side, right_side, left_dim, right_dim):
    return lax.dot_general(
        left_side,
        right_side,
        (((left_dim,), (right_dim,)), ((), ())),
        preferred_element_type=jnp.float32,
    )


def params(limit=VMEM_LIMIT):
    return pltpu.CompilerParams(vmem_limit_bytes=limit)


def cost(flops, nbytes):
    return pl.CostEstimate(flops=int(flops), bytes_accessed=int(nbytes), transcendentals=0)


def tile_of(width, most):
    tile = 128
    for count in range(1, width // 128 + 1):
        if width % (count * 128) == 0 and count * 128 <= most:
            tile = count * 128
    return tile


def pick_kernel(order, pieces, *refs):
    if order is None:
        order, refs = [refs[0][s] for s in range(pieces)], refs[1:]
    ids_ref, weights_ref, tok_ref, grad_ref = refs[:4]
    outs, (sel, scale) = refs[4 : 4 + pieces], refs[4 + pieces :]
    rows = tok_ref.shape[0]
    own_slot = lax.axis_index("expert")

    @pl.when(pl.program_id(0) == 0)
    def _():
        ids = ids_ref[...]
        weights = weights_ref[...]
        earlier = (
            lax.broadcasted_iota(jnp.int32, (rows, rows), 0)
            < lax.broadcasted_iota(jnp.int32, (rows, rows), 1)
        ).astype(jnp.bfloat16)
        want_count = 2 * pieces
        place = lax.broadcasted_iota(jnp.int32, (want_count, rows), 0)
        hits = jnp.zeros((want_count, rows), jnp.float32)
        shares = []
        for piece in range(pieces):
            slot = jnp.bitwise_xor(own_slot, piece)
            source = jnp.int32(0)
            for target in range(pieces):
                source = jnp.where(slot == target, order[target], source)
            for role, expert in enumerate((slot, source)):
                named = ids == expert
                hit = jnp.max(jnp.where(named, 1.0, 0.0), axis=0, keepdims=True)
                hits = jnp.where(place == 2 * piece + role, hit, hits)
                shares.append(jnp.sum(jnp.where(named, weights, 0.0), axis=0, keepdims=True))
        ranks = dot(hits.astype(jnp.bfloat16), earlier, 1, 0)
        ranks = jnp.where(hits > 0.0, ranks, -1.0).astype(jnp.int32)
        row = lax.broadcasted_iota(jnp.int32, (PIECE, rows), 0)
        of_role = jnp.where(row >= 2 * CAP, row - 2 * CAP, row)
        is_grad = of_role >= CAP
        copy = jnp.where(is_grad, of_role - CAP, of_role)
        for piece in range(pieces):
            first, second = 2 * piece, 2 * piece + 1
            is_first = row < 2 * CAP
            rank = jnp.where(is_first, ranks[first : first + 1], ranks[second : second + 1])
            share = jnp.where(is_first, shares[first], shares[second])
            match = jnp.logical_and(copy == rank, row < 4 * CAP)
            part = pl.ds(piece * PIECE, PIECE)
            sel[0, part] = jnp.where(jnp.logical_and(match, jnp.logical_not(is_grad)), 1.0, 0.0)
            sel[1, part] = jnp.where(jnp.logical_and(match, is_grad), 1.0, 0.0)
            scale[part] = jnp.sum(jnp.where(match, share, 0.0), axis=1, keepdims=True)

    token_part = dot(sel[0].astype(jnp.bfloat16), tok_ref[...], 1, 0)
    grad_part = dot(sel[1].astype(jnp.bfloat16), grad_ref[...], 1, 0)
    picked = token_part + scale[...] * grad_part
    for piece in range(pieces):
        outs[piece][...] = picked[piece * PIECE : (piece + 1) * PIECE].astype(jnp.bfloat16)


def pick_rows(order, tokens, grad_out, route_weights, expert_ids):
    pieces = len(order)
    rows, width = tokens.shape
    top = expert_ids.shape[1]
    total = pieces * PIECE
    tile = tile_of(width, 1792)
    known = all(isinstance(s, int) for s in order)
    return pl.pallas_call(
        functools.partial(pick_kernel, tuple(order) if known else None, pieces),
        grid_spec=pltpu.PrefetchScalarGridSpec(
            num_scalar_prefetch=0 if known else 1,
            grid=(width // tile,),
            in_specs=[
                pl.BlockSpec((top, rows), lambda j, *_: (0, 0)),
                pl.BlockSpec((top, rows), lambda j, *_: (0, 0)),
                pl.BlockSpec((rows, tile), lambda j, *_: (0, j)),
                pl.BlockSpec((rows, tile), lambda j, *_: (0, j)),
            ],
            out_specs=[pl.BlockSpec((PIECE, tile), lambda j, *_: (0, j))] * pieces,
            scratch_shapes=[
                pltpu.VMEM((2, total, rows), jnp.float32),
                pltpu.VMEM((total, 1), jnp.float32),
            ],
        ),
        out_shape=[jax.ShapeDtypeStruct((PIECE, width), jnp.bfloat16)] * pieces,
        compiler_params=params(),
        cost_estimate=cost(4 * total * rows * width, 4 * rows * width),
        name="pick_rows",
    )(*(() if known else (jnp.stack(order),)), expert_ids.T, route_weights.T, tokens, grad_out)


def join_kernel(pieces, *refs):
    ins, (own_ref, new_ref) = refs[:pieces], refs[pieces:]
    half = pieces * CAP
    own_slot = lax.axis_index("expert")
    shape = (4 * half, pieces * PIECE)
    row = lax.broadcasted_iota(jnp.int32, shape, 0)
    column = lax.broadcasted_iota(jnp.int32, shape, 1)
    is_second = row >= 2 * half
    of_role = jnp.where(is_second, row - 2 * half, row)
    is_grad = of_role >= half
    in_half = jnp.where(is_grad, of_role - half, of_role)
    chosen = jnp.zeros(shape, jnp.float32)
    for mask in range(pieces):
        copy = in_half - jnp.bitwise_xor(own_slot, mask) * CAP
        wanted = copy + jnp.where(is_grad, CAP, 0) + jnp.where(is_second, 2 * CAP, 0) + mask * PIECE
        mine = jnp.logical_and(copy >= 0, copy < CAP)
        chosen = chosen + jnp.where(jnp.logical_and(mine, column == wanted), 1.0, 0.0)
    rows = jnp.concatenate([ref[...] for ref in ins], axis=0)
    both = dot(chosen.astype(jnp.bfloat16), rows, 1, 0)
    own_ref[...] = both[: 2 * half].astype(jnp.bfloat16)
    new_ref[...] = both[2 * half :].astype(jnp.bfloat16)


def join_pieces(arrays):
    pieces, width = len(arrays), arrays[0].shape[1]
    total = 2 * pieces * CAP
    tile = tile_of(width, 1792)
    return pl.pallas_call(
        functools.partial(join_kernel, pieces),
        grid=(width // tile,),
        in_specs=[pl.BlockSpec((PIECE, tile), lambda j: (0, j))] * pieces,
        out_specs=[pl.BlockSpec((total, tile), lambda j: (0, j))] * 2,
        out_shape=[jax.ShapeDtypeStruct((total, width), jnp.bfloat16)] * 2,
        compiler_params=params(),
        cost_estimate=cost(4 * total * PIECE * pieces * width, 8 * total * width),
        name="join_pieces",
    )(*arrays)


def joined(refs):
    return refs[0][...] if len(refs) == 1 else jnp.concatenate([ref[...] for ref in refs], axis=0)


def parts_spec(parts, tile):
    return [pl.BlockSpec((part.shape[0], tile), lambda j: (0, j)) for part in parts]


def factor_kernel(half, *refs):
    (w_in_ref, w_down_ref, out_ref, acc), x_refs = refs[-4:], refs[:-4]
    step = pl.program_id(0)
    count, units = acc.shape[0], w_down_ref.shape[1]

    @pl.when(step == 0)
    def _():
        acc[...] = jnp.zeros_like(acc)

    x = joined(x_refs)
    acc[:, 0:units] += dot(x, w_in_ref[0, 0], 1, 1)
    acc[:, units : 2 * units] += dot(x, w_in_ref[0, 1], 1, 1)
    acc[:, 2 * units : 3 * units] += dot(x, w_down_ref[0], 1, 1)

    @pl.when(step == pl.num_programs(0) - 1)
    def _():
        gate = acc[:, 0:units]
        up = acc[:, units : 2 * units]
        back = pltpu.roll(acc[:, 2 * units : 3 * units], count - half, 0)
        sig = jax.nn.sigmoid(gate)
        activated = gate * sig
        slopes = sig * (1.0 + gate * (1.0 - sig))
        hidden = pltpu.roll(activated * up, half, 0)
        is_token = lax.broadcasted_iota(jnp.int32, (count, units), 0) % (2 * half) < half
        out_ref[:, 0:units] = jnp.where(is_token, back * up * slopes, hidden).astype(jnp.bfloat16)
        out_ref[:, units : 2 * units] = jnp.where(is_token, back * activated, 0.0).astype(jnp.bfloat16)


def factors_of(parts, w_in, w_down, half):
    count, width = sum(part.shape[0] for part in parts), parts[0].shape[1]
    units = w_down.shape[1]
    tile = tile_of(width, 896)
    return pl.pallas_call(
        functools.partial(factor_kernel, half),
        grid=(width // tile,),
        in_specs=[
            *parts_spec(parts, tile),
            pl.BlockSpec((1, 2, units, tile), lambda j: (0, 0, 0, j)),
            pl.BlockSpec((1, units, tile), lambda j: (0, 0, j)),
        ],
        out_specs=pl.BlockSpec((count, 2 * units), lambda j: (0, 0)),
        out_shape=jax.ShapeDtypeStruct((count, 2 * units), jnp.bfloat16),
        scratch_shapes=[pltpu.VMEM((count, 3 * units), jnp.float32)],
        compiler_params=params(),
        cost_estimate=cost(6 * count * units * width, 6 * units * width + 2 * count * width),
        name="factors",
    )(*parts, w_in, w_down)


def new_rows_of(crossing, x_refs):
    if crossing is None:
        return joined(x_refs)
    own_slot = lax.axis_index("expert")
    gathered = functools.reduce(jnp.logical_or, [own_slot == slot for slot in crossing])
    return jnp.where(gathered, joined(x_refs[:-1]), x_refs[-1][...])


def grad_kernel(half, crossing, factor_ref, *refs):
    (out_ref, turned), x_refs = refs[-2:], refs[:-2]
    units = out_ref.shape[2]

    @pl.when(pl.program_id(0) == 0)
    def _():
        is_token = lax.broadcasted_iota(jnp.int32, factor_ref.shape, 0) % (2 * half) < half
        both = factor_ref[...].astype(jnp.float32)
        turned[...] = jnp.where(is_token, both, 0.0).T.astype(jnp.bfloat16)

    grads = dot(turned[...], new_rows_of(crossing, x_refs), 1, 0)
    out_ref[0, 0] = grads[:units].astype(jnp.bfloat16)
    out_ref[0, 1] = grads[units:].astype(jnp.bfloat16)


def grads_of(factors, crossing, parts, half):
    count, width = factors.shape[0], parts[0].shape[1]
    units = factors.shape[1] // 2
    tile = tile_of(width, 896)
    return pl.pallas_call(
        functools.partial(grad_kernel, half, crossing),
        grid=(width // tile,),
        in_specs=[
            pl.BlockSpec((count, 2 * units), lambda j: (0, 0)),
            *parts_spec(parts, tile),
        ],
        out_specs=pl.BlockSpec((1, 2, units, tile), lambda j: (0, 0, 0, j)),
        out_shape=jax.ShapeDtypeStruct((1, 2, units, width), jnp.bfloat16),
        scratch_shapes=[pltpu.VMEM((2 * units, count), jnp.bfloat16)],
        compiler_params=params(),
        cost_estimate=cost(4 * count * units * width, 4 * units * width + 2 * count * width),
        name="in_grads",
    )(factors, *parts)


def pack_kernel(*refs):
    for number, ref in enumerate(refs[:-1]):
        refs[-1][number] = ref[0].astype(jnp.bfloat16)


def pack(*arrays):
    _, units, width = arrays[0].shape
    count = len(arrays)
    tile = tile_of(width, 896)
    return pl.pallas_call(
        pack_kernel,
        grid=(width // tile,),
        in_specs=[pl.BlockSpec((1, units, tile), lambda j: (0, 0, j))] * count,
        out_specs=pl.BlockSpec((count, units, tile), lambda j: (0, 0, j)),
        out_shape=jax.ShapeDtypeStruct((count, units, width), jnp.bfloat16),
        compiler_params=params(),
        cost_estimate=cost(2 * units * width, 16 * units * width),
        name="pack_state",
    )(*arrays)


def adam_kernel(half, crossing, factor_ref, state_ref, *refs):
    (down_ref, one_ref, two_ref, turned), x_refs = refs[-4:], refs[:-4]
    count, units = factor_ref.shape[0], down_ref.shape[1]

    @pl.when(pl.program_id(0) == 0)
    def _():
        is_token = lax.broadcasted_iota(jnp.int32, (count, units), 0) % (2 * half) < half
        both = factor_ref[:, :units].astype(jnp.float32)
        turned[...] = jnp.where(is_token, 0.0, both).T.astype(jnp.bfloat16)

    down_grad = dot(turned[...], new_rows_of(crossing, x_refs), 1, 0)
    w_down, moment1, moment2 = [state_ref[k].astype(jnp.float32) for k in range(3)]
    rate = adam_rate / (1.0 - beta_one**adam_step)
    fix_two = 1.0 / (1.0 - beta_two**adam_step)
    first_new = beta_one * moment1 + (1.0 - beta_one) * down_grad
    second_new = beta_two * moment2 + (1.0 - beta_two) * (down_grad * down_grad)
    change = rate * first_new / (jnp.sqrt(second_new * fix_two) + adam_eps)
    down_ref[0] = (w_down - change).astype(jnp.bfloat16)
    one_ref[0] = first_new
    two_ref[0] = second_new


def adam(factors, crossing, parts, state, half):
    count = factors.shape[0]
    _, units, width = state.shape
    tile = tile_of(width, 512)
    spec = pl.BlockSpec((1, units, tile), lambda j: (0, 0, j))
    return pl.pallas_call(
        functools.partial(adam_kernel, half, crossing),
        grid=(width // tile,),
        in_specs=[
            pl.BlockSpec((count, 2 * units), lambda j: (0, 0)),
            pl.BlockSpec((3, units, tile), lambda j: (0, 0, j)),
            *parts_spec(parts, tile),
        ],
        out_specs=[spec, spec, spec],
        out_shape=[
            jax.ShapeDtypeStruct((1, units, width), kind) for kind in (jnp.bfloat16, jnp.float32, jnp.float32)
        ],
        scratch_shapes=[pltpu.VMEM((units, count), jnp.bfloat16)],
        compiler_params=params(),
        cost_estimate=cost(2 * count * units * width, 16 * units * width + 2 * count * width),
        name="adam",
    )(factors, state, *parts)


def gather_dp(block, columns, slots=None):
    size = lax.axis_size("dp")
    planes = size // columns

    def crossed(array, mask):
        if slots is None:
            return lax.ppermute(array, "dp", [(i, i ^ mask) for i in range(size)])
        pairs = [(s * size + i, s * size + (i ^ mask)) for s in slots for i in range(size)]
        return lax.ppermute(array, ("expert", "dp"), pairs)

    blocks = [block] + [crossed(block, k * columns) for k in range(1, planes)]
    near = jnp.concatenate(blocks[: planes // 2], axis=0)
    far = jnp.concatenate(blocks[planes // 2 :], axis=0)
    return [near, far] + [crossed(p, k) for k in range(1, columns) for p in (near, far)]


def after(array, *others):
    return lax.optimization_barrier((array, *others))[0]


def section_swaps(swap_code, slot, sections):
    swaps = []
    for bit in range(sections):
        lower = jnp.minimum(slot, jnp.bitwise_xor(slot, 1 << bit))
        swaps.append(swap_code[lower] // (1 << bit) % 2 == 1)
    return swaps


def static_order(expert_count, sections, swapped_pairs):
    order = list(range(expert_count))
    for bit in range(sections):
        step = [s ^ (1 << bit) if (bit, min(s, s ^ (1 << bit))) in swapped_pairs else s for s in range(expert_count)]
        order = [order[s] for s in step]
    return order


def layer(move, columns, order, operands):
    tokens, grad_out, route_weights, expert_ids, w_in, w_down, moment1, moment2 = operands
    expert_count = len(order)
    half = expert_count * CAP
    crossing = None
    if all(isinstance(slot, int) for slot in order):
        crossing = [s for s in range(expert_count) if order[s] not in (s, s ^ 1)]
    if crossing is not None and len(crossing) == expert_count:
        crossing = None

    picked = pick_rows(order, tokens, grad_out, route_weights, expert_ids)
    arrived = [picked[0]]
    for mask in range(1, expert_count):
        pairs = [(i, i ^ mask) for i in range(expert_count)]
        arrived.append(lax.ppermute(picked[mask], "expert", pairs))
    state = move(pack(after(w_down, picked[0]), moment1, moment2))
    own_block, new_block = join_pieces(arrived)
    own_parts = gather_dp(own_block, columns)
    factors = factors_of(own_parts, w_in, w_down, half)
    new_parts = gather_dp(after(new_block, *own_parts[:2]), columns, crossing)
    if crossing is not None:
        pairs = [(order[s], s) for s in range(expert_count) if s not in crossing]
        new_parts.append(lax.ppermute(jnp.concatenate(own_parts, axis=0), "expert", pairs))
    factors = move(factors)
    grads = grads_of(factors, crossing, new_parts, half)
    return (*adam(factors, crossing, new_parts, state, half), grads)


def local(tokens, grad_out, route_weights, expert_ids, swap_code, w_in, w_down, moment1, moment2):
    expert_count = lax.axis_size("expert")
    sections = expert_count.bit_length() - 1
    columns = max(1, expert_count // 2)
    operands = (tokens, grad_out, route_weights, expert_ids, w_in, w_down, moment1, moment2)

    free = [(b, s) for b in range(sections) for s in range(1, expert_count) if not s >> b & 1]
    fixed = [(b, 0) for b in range(sections)]
    if len(free) <= 2:
        branches = []
        for taken in itertools.product((False, True), repeat=len(free)):
            pairs = fixed + [pair for pair, yes in zip(free, taken) if yes]
            order = static_order(expert_count, sections, pairs)
            move = functools.partial(
                lax.ppermute, axis_name="expert", perm=[(order[s], s) for s in range(expert_count)]
            )
            branches.append(functools.partial(layer, move, columns, order))
        which = jnp.int32(0)
        for bit, slot in free:
            which = which * 2 + ((swap_code[slot] >> bit) & 1)
        return lax.switch(which, branches, operands)

    swaps = section_swaps(swap_code, lax.axis_index("expert"), sections)

    def move_by_sections(array):
        for bit in range(sections):
            pairs = [(i, i ^ (1 << bit)) for i in range(expert_count)]
            array = jnp.where(swaps[bit], lax.ppermute(array, "expert", pairs), array)
        return array

    slots = jnp.arange(expert_count, dtype=jnp.int32)
    order = slots
    for bit in range(sections):
        partner = jnp.bitwise_xor(slots, 1 << bit)
        swapped = swap_code[jnp.minimum(slots, partner)] // (1 << bit) % 2 == 1
        order = order[jnp.where(swapped, partner, slots)]
    return layer(move_by_sections, columns, [order[s] for s in range(expert_count)], operands)


def solution(mesh):
    placed = (
        P(("expert", "dp"), None),
        P(("expert", "dp"), None),
        P(("expert", "dp"), None),
        P(("expert", "dp"), None),
        P(),
        P("expert", None, "dp", None),
        P("expert", "dp", None),
        P("expert", "dp", None),
        P("expert", "dp", None),
    )
    return jax.shard_map(
        local,
        mesh=mesh,
        in_specs=placed,
        out_specs=(
            P("expert", "dp", None),
            P("expert", "dp", None),
            P("expert", "dp", None),
            P("expert", None, "dp", None),
        ),
        check_vma=False,
    )
```

```python
import functools
import itertools

import jax
import jax.numpy as jnp
from jax import lax
from jax.experimental import pallas as pl
from jax.experimental.pallas import tpu as pltpu
from jax.sharding import PartitionSpec as P

CAP = 5
PIECE = 24
VMEM_LIMIT = 60 * 1024 * 1024

adam_rate = 0.01
beta_one = 0.9
beta_two = 0.999
adam_step = 100.0
adam_eps = 1e-08


def dot(left_side, right_side, left_dim, right_dim):
    return lax.dot_general(
        left_side,
        right_side,
        (((left_dim,), (right_dim,)), ((), ())),
        preferred_element_type=jnp.float32,
    )


def params(limit=VMEM_LIMIT):
    return pltpu.CompilerParams(vmem_limit_bytes=limit)


def cost(flops, nbytes):
    return pl.CostEstimate(flops=int(flops), bytes_accessed=int(nbytes), transcendentals=0)


def tile_of(width, most):
    tile = 128
    for count in range(1, width // 128 + 1):
        if width % (count * 128) == 0 and count * 128 <= most:
            tile = count * 128
    return tile


def pick_kernel(order, pieces, *refs):
    if order is None:
        order, refs = [refs[0][s] for s in range(pieces)], refs[1:]
    ids_ref, weights_ref, tok_ref, grad_ref = refs[:4]
    outs, (sel, scale) = refs[4 : 4 + pieces], refs[4 + pieces :]
    rows = tok_ref.shape[0]
    own_slot = lax.axis_index("expert")

    @pl.when(pl.program_id(0) == 0)
    def _():
        ids = ids_ref[...]
        weights = weights_ref[...]
        earlier = (
            lax.broadcasted_iota(jnp.int32, (rows, rows), 0)
            < lax.broadcasted_iota(jnp.int32, (rows, rows), 1)
        ).astype(jnp.bfloat16)
        want_count = 2 * pieces
        place = lax.broadcasted_iota(jnp.int32, (want_count, rows), 0)
        hits = jnp.zeros((want_count, rows), jnp.float32)
        shares = []
        for piece in range(pieces):
            slot = jnp.bitwise_xor(own_slot, piece)
            source = jnp.int32(0)
            for target in range(pieces):
                source = jnp.where(slot == target, order[target], source)
            for role, expert in enumerate((slot, source)):
                named = ids == expert
                hit = jnp.max(jnp.where(named, 1.0, 0.0), axis=0, keepdims=True)
                hits = jnp.where(place == 2 * piece + role, hit, hits)
                shares.append(jnp.sum(jnp.where(named, weights, 0.0), axis=0, keepdims=True))
        ranks = dot(hits.astype(jnp.bfloat16), earlier, 1, 0)
        ranks = jnp.where(hits > 0.0, ranks, -1.0).astype(jnp.int32)
        row = lax.broadcasted_iota(jnp.int32, (PIECE, rows), 0)
        of_role = jnp.where(row >= 2 * CAP, row - 2 * CAP, row)
        is_grad = of_role >= CAP
        copy = jnp.where(is_grad, of_role - CAP, of_role)
        for piece in range(pieces):
            first, second = 2 * piece, 2 * piece + 1
            is_first = row < 2 * CAP
            rank = jnp.where(is_first, ranks[first : first + 1], ranks[second : second + 1])
            share = jnp.where(is_first, shares[first], shares[second])
            match = jnp.logical_and(copy == rank, row < 4 * CAP)
            part = pl.ds(piece * PIECE, PIECE)
            sel[0, part] = jnp.where(jnp.logical_and(match, jnp.logical_not(is_grad)), 1.0, 0.0)
            sel[1, part] = jnp.where(jnp.logical_and(match, is_grad), 1.0, 0.0)
            scale[part] = jnp.sum(jnp.where(match, share, 0.0), axis=1, keepdims=True)

    token_part = dot(sel[0].astype(jnp.bfloat16), tok_ref[...], 1, 0)
    grad_part = dot(sel[1].astype(jnp.bfloat16), grad_ref[...], 1, 0)
    picked = token_part + scale[...] * grad_part
    for piece in range(pieces):
        outs[piece][...] = picked[piece * PIECE : (piece + 1) * PIECE].astype(jnp.bfloat16)


def pick_rows(order, tokens, grad_out, route_weights, expert_ids):
    pieces = len(order)
    rows, width = tokens.shape
    top = expert_ids.shape[1]
    total = pieces * PIECE
    tile = tile_of(width, 1792)
    known = all(isinstance(s, int) for s in order)
    return pl.pallas_call(
        functools.partial(pick_kernel, tuple(order) if known else None, pieces),
        grid_spec=pltpu.PrefetchScalarGridSpec(
            num_scalar_prefetch=0 if known else 1,
            grid=(width // tile,),
            in_specs=[
                pl.BlockSpec((top, rows), lambda j, *_: (0, 0)),
                pl.BlockSpec((top, rows), lambda j, *_: (0, 0)),
                pl.BlockSpec((rows, tile), lambda j, *_: (0, j)),
                pl.BlockSpec((rows, tile), lambda j, *_: (0, j)),
            ],
            out_specs=[pl.BlockSpec((PIECE, tile), lambda j, *_: (0, j))] * pieces,
            scratch_shapes=[
                pltpu.VMEM((2, total, rows), jnp.float32),
                pltpu.VMEM((total, 1), jnp.float32),
            ],
        ),
        out_shape=[jax.ShapeDtypeStruct((PIECE, width), jnp.bfloat16)] * pieces,
        compiler_params=params(),
        cost_estimate=cost(4 * total * rows * width, 4 * rows * width),
        name="pick_rows",
    )(*(() if known else (jnp.stack(order),)), expert_ids.T, route_weights.T, tokens, grad_out)


def join_kernel(pieces, *refs):
    ins, (own_ref, new_ref) = refs[:pieces], refs[pieces:]
    half = pieces * CAP
    own_slot = lax.axis_index("expert")
    shape = (4 * half, pieces * PIECE)
    row = lax.broadcasted_iota(jnp.int32, shape, 0)
    column = lax.broadcasted_iota(jnp.int32, shape, 1)
    is_second = row >= 2 * half
    of_role = jnp.where(is_second, row - 2 * half, row)
    is_grad = of_role >= half
    in_half = jnp.where(is_grad, of_role - half, of_role)
    chosen = jnp.zeros(shape, jnp.float32)
    for mask in range(pieces):
        copy = in_half - jnp.bitwise_xor(own_slot, mask) * CAP
        wanted = copy + jnp.where(is_grad, CAP, 0) + jnp.where(is_second, 2 * CAP, 0) + mask * PIECE
        mine = jnp.logical_and(copy >= 0, copy < CAP)
        chosen = chosen + jnp.where(jnp.logical_and(mine, column == wanted), 1.0, 0.0)
    rows = jnp.concatenate([ref[...] for ref in ins], axis=0)
    both = dot(chosen.astype(jnp.bfloat16), rows, 1, 0)
    own_ref[...] = both[: 2 * half].astype(jnp.bfloat16)
    new_ref[...] = both[2 * half :].astype(jnp.bfloat16)


def join_pieces(arrays):
    pieces, width = len(arrays), arrays[0].shape[1]
    total = 2 * pieces * CAP
    tile = tile_of(width, 1792)
    return pl.pallas_call(
        functools.partial(join_kernel, pieces),
        grid=(width // tile,),
        in_specs=[pl.BlockSpec((PIECE, tile), lambda j: (0, j))] * pieces,
        out_specs=[pl.BlockSpec((total, tile), lambda j: (0, j))] * 2,
        out_shape=[jax.ShapeDtypeStruct((total, width), jnp.bfloat16)] * 2,
        compiler_params=params(),
        cost_estimate=cost(4 * total * PIECE * pieces * width, 8 * total * width),
        name="join_pieces",
    )(*arrays)


def rows_apart(refs, half):
    blocks = [(ref, first) for ref in refs for first in range(0, ref.shape[0], 2 * half)]
    token_rows = jnp.concatenate([ref[first : first + half] for ref, first in blocks], axis=0)
    grad_rows = jnp.concatenate([ref[first + half : first + 2 * half] for ref, first in blocks], axis=0)
    return token_rows, grad_rows


def parts_spec(parts, tile):
    return [pl.BlockSpec((part.shape[0], tile), lambda j: (0, j)) for part in parts]


def factor_kernel(half, *refs):
    (w_in_ref, w_down_ref, out_ref, acc), x_refs = refs[-4:], refs[:-4]
    step = pl.program_id(0)
    units = w_down_ref.shape[1]

    @pl.when(step == 0)
    def _():
        acc[...] = jnp.zeros_like(acc)

    token_rows, grad_rows = rows_apart(x_refs, half)
    acc[0] += dot(token_rows, w_in_ref[0, 0], 1, 1)
    acc[1] += dot(token_rows, w_in_ref[0, 1], 1, 1)
    acc[2] += dot(grad_rows, w_down_ref[0], 1, 1)

    @pl.when(step == pl.num_programs(0) - 1)
    def _():
        gate, up, back = acc[0], acc[1], acc[2]
        sig = jax.nn.sigmoid(gate)
        activated = gate * sig
        slopes = sig * (1.0 + gate * (1.0 - sig))
        out_ref[:, 0:units] = (back * up * slopes).astype(jnp.bfloat16)
        out_ref[:, units : 2 * units] = (back * activated).astype(jnp.bfloat16)
        out_ref[:, 2 * units : 3 * units] = (activated * up).astype(jnp.bfloat16)


def factors_of(parts, w_in, w_down, half):
    count, width = sum(part.shape[0] for part in parts) // 2, parts[0].shape[1]
    units = w_down.shape[1]
    tile = tile_of(width, 896)
    return pl.pallas_call(
        functools.partial(factor_kernel, half),
        grid=(width // tile,),
        in_specs=[
            *parts_spec(parts, tile),
            pl.BlockSpec((1, 2, units, tile), lambda j: (0, 0, 0, j)),
            pl.BlockSpec((1, units, tile), lambda j: (0, 0, j)),
        ],
        out_specs=pl.BlockSpec((count, 3 * units), lambda j: (0, 0)),
        out_shape=jax.ShapeDtypeStruct((count, 3 * units), jnp.bfloat16),
        scratch_shapes=[pltpu.VMEM((3, count, units), jnp.float32)],
        compiler_params=params(),
        cost_estimate=cost(6 * count * units * width, 6 * units * width + 4 * count * width),
        name="factors",
    )(*parts, w_in, w_down)


def pack_kernel(*refs):
    for number, ref in enumerate(refs[:-1]):
        refs[-1][number] = ref[0].astype(jnp.bfloat16)


def pack(*arrays):
    _, units, width = arrays[0].shape
    count = len(arrays)
    tile = tile_of(width, 896)
    return pl.pallas_call(
        pack_kernel,
        grid=(width // tile,),
        in_specs=[pl.BlockSpec((1, units, tile), lambda j: (0, 0, j))] * count,
        out_specs=pl.BlockSpec((count, units, tile), lambda j: (0, 0, j)),
        out_shape=jax.ShapeDtypeStruct((count, units, width), jnp.bfloat16),
        compiler_params=params(),
        cost_estimate=cost(2 * units * width, 16 * units * width),
        name="pack_state",
    )(*arrays)


def finish_kernel(half, crossing, factor_ref, state_ref, *refs):
    (down_ref, one_ref, two_ref, grad_ref, turned), x_refs = refs[-5:], refs[:-5]
    units = down_ref.shape[1]

    @pl.when(pl.program_id(0) == 0)
    def _():
        turned[...] = factor_ref[...].astype(jnp.float32).T.astype(jnp.bfloat16)

    if crossing is None:
        token_rows, grad_rows = rows_apart(x_refs, half)
    else:
        own_slot = lax.axis_index("expert")
        gathered = functools.reduce(jnp.logical_or, [own_slot == slot for slot in crossing])
        pairs = zip(rows_apart(x_refs[:-1], half), rows_apart(x_refs[-1:], half))
        token_rows, grad_rows = [jnp.where(gathered, theirs, mine) for theirs, mine in pairs]
    in_grads = dot(turned[: 2 * units], token_rows, 1, 0).astype(jnp.bfloat16)
    grad_ref[0, 0] = in_grads[:units]
    grad_ref[0, 1] = in_grads[units:]
    down_grad = dot(turned[2 * units :], grad_rows, 1, 0)
    w_down, moment1, moment2 = [state_ref[k].astype(jnp.float32) for k in range(3)]
    rate = adam_rate / (1.0 - beta_one**adam_step)
    fix_two = 1.0 / (1.0 - beta_two**adam_step)
    first_new = beta_one * moment1 + (1.0 - beta_one) * down_grad
    second_new = beta_two * moment2 + (1.0 - beta_two) * (down_grad * down_grad)
    change = rate * first_new / (jnp.sqrt(second_new * fix_two) + adam_eps)
    down_ref[0] = (w_down - change).astype(jnp.bfloat16)
    one_ref[0] = first_new
    two_ref[0] = second_new


def finish(factors, crossing, parts, state, half):
    count = factors.shape[0]
    _, units, width = state.shape
    tile = tile_of(width, 512)
    spec = pl.BlockSpec((1, units, tile), lambda j: (0, 0, j))
    kinds = (jnp.bfloat16, jnp.float32, jnp.float32)
    return pl.pallas_call(
        functools.partial(finish_kernel, half, crossing),
        grid=(width // tile,),
        in_specs=[
            pl.BlockSpec((count, 3 * units), lambda j: (0, 0)),
            pl.BlockSpec((3, units, tile), lambda j: (0, 0, j)),
            *parts_spec(parts, tile),
        ],
        out_specs=[spec, spec, spec, pl.BlockSpec((1, 2, units, tile), lambda j: (0, 0, 0, j))],
        out_shape=[jax.ShapeDtypeStruct((1, units, width), kind) for kind in kinds]
        + [jax.ShapeDtypeStruct((1, 2, units, width), jnp.bfloat16)],
        scratch_shapes=[pltpu.VMEM((3 * units, count), jnp.bfloat16)],
        compiler_params=params(),
        cost_estimate=cost(6 * count * units * width, 20 * units * width + 4 * count * width),
        name="finish",
    )(factors, state, *parts)


def gather_dp(block, columns, slots=None):
    size = lax.axis_size("dp")
    planes = size // columns

    def crossed(array, mask):
        if slots is None:
            return lax.ppermute(array, "dp", [(i, i ^ mask) for i in range(size)])
        pairs = [(s * size + i, s * size + (i ^ mask)) for s in slots for i in range(size)]
        return lax.ppermute(array, ("expert", "dp"), pairs)

    blocks = [block] + [crossed(block, k * columns) for k in range(1, planes)]
    near = jnp.concatenate(blocks[: planes // 2], axis=0)
    far = jnp.concatenate(blocks[planes // 2 :], axis=0)
    return [near, far] + [crossed(p, k) for k in range(1, columns) for p in (near, far)]


def after(array, *others):
    return lax.optimization_barrier((array, *others))[0]


def section_swaps(swap_code, slot, sections):
    swaps = []
    for bit in range(sections):
        lower = jnp.minimum(slot, jnp.bitwise_xor(slot, 1 << bit))
        swaps.append(swap_code[lower] // (1 << bit) % 2 == 1)
    return swaps


def static_order(expert_count, sections, swapped_pairs):
    order = list(range(expert_count))
    for bit in range(sections):
        step = [s ^ (1 << bit) if (bit, min(s, s ^ (1 << bit))) in swapped_pairs else s for s in range(expert_count)]
        order = [order[s] for s in step]
    return order


def layer(move, columns, order, operands):
    tokens, grad_out, route_weights, expert_ids, w_in, w_down, moment1, moment2 = operands
    expert_count = len(order)
    half = expert_count * CAP
    crossing = None
    if all(isinstance(slot, int) for slot in order):
        crossing = [s for s in range(expert_count) if order[s] not in (s, s ^ 1)]
    if crossing is not None and len(crossing) == expert_count:
        crossing = None

    picked = pick_rows(order, tokens, grad_out, route_weights, expert_ids)
    arrived = [picked[0]]
    for mask in range(1, expert_count):
        pairs = [(i, i ^ mask) for i in range(expert_count)]
        arrived.append(lax.ppermute(picked[mask], "expert", pairs))
    state = move(after(pack(after(w_down, picked[0]), moment1, moment2), *arrived[1:]))
    own_block, new_block = join_pieces(arrived)
    own_parts = gather_dp(own_block, columns)
    factors = factors_of(own_parts, w_in, w_down, half)
    new_parts = gather_dp(after(new_block, *own_parts[:2]), columns, crossing)
    if crossing is not None:
        pairs = [(order[s], s) for s in range(expert_count) if s not in crossing]
        new_parts.append(lax.ppermute(jnp.concatenate(own_parts, axis=0), "expert", pairs))
    factors = move(factors)
    return tuple(finish(factors, crossing, new_parts, state, half))


def local(tokens, grad_out, route_weights, expert_ids, swap_code, w_in, w_down, moment1, moment2):
    expert_count = lax.axis_size("expert")
    sections = expert_count.bit_length() - 1
    columns = max(1, expert_count // 2)
    operands = (tokens, grad_out, route_weights, expert_ids, w_in, w_down, moment1, moment2)

    free = [(b, s) for b in range(sections) for s in range(1, expert_count) if not s >> b & 1]
    fixed = [(b, 0) for b in range(sections)]
    if len(free) <= 2:
        branches = []
        for taken in itertools.product((False, True), repeat=len(free)):
            pairs = fixed + [pair for pair, yes in zip(free, taken) if yes]
            order = static_order(expert_count, sections, pairs)
            move = functools.partial(
                lax.ppermute, axis_name="expert", perm=[(order[s], s) for s in range(expert_count)]
            )
            branches.append(functools.partial(layer, move, columns, order))
        which = jnp.int32(0)
        for bit, slot in free:
            which = which * 2 + ((swap_code[slot] >> bit) & 1)
        return lax.switch(which, branches, operands)

    swaps = section_swaps(swap_code, lax.axis_index("expert"), sections)

    def move_by_sections(array):
        for bit in range(sections):
            pairs = [(i, i ^ (1 << bit)) for i in range(expert_count)]
            array = jnp.where(swaps[bit], lax.ppermute(array, "expert", pairs), array)
        return array

    slots = jnp.arange(expert_count, dtype=jnp.int32)
    order = slots
    for bit in range(sections):
        partner = jnp.bitwise_xor(slots, 1 << bit)
        swapped = swap_code[jnp.minimum(slots, partner)] // (1 << bit) % 2 == 1
        order = order[jnp.where(swapped, partner, slots)]
    return layer(move_by_sections, columns, [order[s] for s in range(expert_count)], operands)


def solution(mesh):
    placed = (
        P(("expert", "dp"), None),
        P(("expert", "dp"), None),
        P(("expert", "dp"), None),
        P(("expert", "dp"), None),
        P(),
        P("expert", None, "dp", None),
        P("expert", "dp", None),
        P("expert", "dp", None),
        P("expert", "dp", None),
    )
    return jax.shard_map(
        local,
        mesh=mesh,
        in_specs=placed,
        out_specs=(
            P("expert", "dp", None),
            P("expert", "dp", None),
            P("expert", "dp", None),
            P("expert", None, "dp", None),
        ),
        check_vma=False,
    )
```

```python
import functools
import itertools

import jax
import jax.numpy as jnp
from jax import lax
from jax.experimental import pallas as pl
from jax.experimental.pallas import tpu as pltpu
from jax.sharding import PartitionSpec as P

CAP = 5
PIECE = 24
VMEM_LIMIT = 60 * 1024 * 1024

adam_rate = 0.01
beta_one = 0.9
beta_two = 0.999
adam_step = 100.0
adam_eps = 1e-08


def dot(left_side, right_side, left_dim, right_dim):
    return lax.dot_general(
        left_side,
        right_side,
        (((left_dim,), (right_dim,)), ((), ())),
        preferred_element_type=jnp.float32,
    )


def params(limit=VMEM_LIMIT):
    return pltpu.CompilerParams(vmem_limit_bytes=limit)


def cost(flops, nbytes):
    return pl.CostEstimate(flops=int(flops), bytes_accessed=int(nbytes), transcendentals=0)


def tile_of(width, most):
    tile = 128
    for count in range(1, width // 128 + 1):
        if width % (count * 128) == 0 and count * 128 <= most:
            tile = count * 128
    return tile


def pick_kernel(order, pieces, *refs):
    if order is None:
        order, refs = [refs[0][s] for s in range(pieces)], refs[1:]
    ids_ref, weights_ref, tok_ref, grad_ref = refs[:4]
    outs, (sel, scale) = refs[4 : 4 + pieces], refs[4 + pieces :]
    rows = tok_ref.shape[0]
    own_slot = lax.axis_index("expert")

    @pl.when(pl.program_id(0) == 0)
    def _():
        ids = ids_ref[...]
        weights = weights_ref[...]
        earlier = (
            lax.broadcasted_iota(jnp.int32, (rows, rows), 0)
            < lax.broadcasted_iota(jnp.int32, (rows, rows), 1)
        ).astype(jnp.bfloat16)
        want_count = 2 * pieces
        place = lax.broadcasted_iota(jnp.int32, (want_count, rows), 0)
        hits = jnp.zeros((want_count, rows), jnp.float32)
        shares = []
        for piece in range(pieces):
            slot = jnp.bitwise_xor(own_slot, piece)
            source = jnp.int32(0)
            for target in range(pieces):
                source = jnp.where(slot == target, order[target], source)
            for role, expert in enumerate((slot, source)):
                named = ids == expert
                hit = jnp.max(jnp.where(named, 1.0, 0.0), axis=0, keepdims=True)
                hits = jnp.where(place == 2 * piece + role, hit, hits)
                shares.append(jnp.sum(jnp.where(named, weights, 0.0), axis=0, keepdims=True))
        ranks = dot(hits.astype(jnp.bfloat16), earlier, 1, 0)
        ranks = jnp.where(hits > 0.0, ranks, -1.0).astype(jnp.int32)
        row = lax.broadcasted_iota(jnp.int32, (PIECE, rows), 0)
        of_role = jnp.where(row >= 2 * CAP, row - 2 * CAP, row)
        is_grad = of_role >= CAP
        copy = jnp.where(is_grad, of_role - CAP, of_role)
        for piece in range(pieces):
            first, second = 2 * piece, 2 * piece + 1
            is_first = row < 2 * CAP
            rank = jnp.where(is_first, ranks[first : first + 1], ranks[second : second + 1])
            share = jnp.where(is_first, shares[first], shares[second])
            match = jnp.logical_and(copy == rank, row < 4 * CAP)
            part = pl.ds(piece * PIECE, PIECE)
            sel[0, part] = jnp.where(jnp.logical_and(match, jnp.logical_not(is_grad)), 1.0, 0.0)
            sel[1, part] = jnp.where(jnp.logical_and(match, is_grad), 1.0, 0.0)
            scale[part] = jnp.sum(jnp.where(match, share, 0.0), axis=1, keepdims=True)

    token_part = dot(sel[0].astype(jnp.bfloat16), tok_ref[...], 1, 0)
    grad_part = dot(sel[1].astype(jnp.bfloat16), grad_ref[...], 1, 0)
    picked = token_part + scale[...] * grad_part
    for piece in range(pieces):
        outs[piece][...] = picked[piece * PIECE : (piece + 1) * PIECE].astype(jnp.bfloat16)


def pick_rows(order, tokens, grad_out, route_weights, expert_ids):
    pieces = len(order)
    rows, width = tokens.shape
    top = expert_ids.shape[1]
    total = pieces * PIECE
    tile = tile_of(width, 1792)
    known = all(isinstance(s, int) for s in order)
    return pl.pallas_call(
        functools.partial(pick_kernel, tuple(order) if known else None, pieces),
        grid_spec=pltpu.PrefetchScalarGridSpec(
            num_scalar_prefetch=0 if known else 1,
            grid=(width // tile,),
            in_specs=[
                pl.BlockSpec((top, rows), lambda j, *_: (0, 0)),
                pl.BlockSpec((top, rows), lambda j, *_: (0, 0)),
                pl.BlockSpec((rows, tile), lambda j, *_: (0, j)),
                pl.BlockSpec((rows, tile), lambda j, *_: (0, j)),
            ],
            out_specs=[pl.BlockSpec((PIECE, tile), lambda j, *_: (0, j))] * pieces,
            scratch_shapes=[
                pltpu.VMEM((2, total, rows), jnp.float32),
                pltpu.VMEM((total, 1), jnp.float32),
            ],
        ),
        out_shape=[jax.ShapeDtypeStruct((PIECE, width), jnp.bfloat16)] * pieces,
        compiler_params=params(),
        cost_estimate=cost(4 * total * rows * width, 4 * rows * width),
        name="pick_rows",
    )(*(() if known else (jnp.stack(order),)), expert_ids.T, route_weights.T, tokens, grad_out)


def join_kernel(pieces, *refs):
    ins, (own_ref, new_ref) = refs[:pieces], refs[pieces:]
    half = pieces * CAP
    own_slot = lax.axis_index("expert")
    shape = (4 * half, pieces * PIECE)
    row = lax.broadcasted_iota(jnp.int32, shape, 0)
    column = lax.broadcasted_iota(jnp.int32, shape, 1)
    is_second = row >= 2 * half
    of_role = jnp.where(is_second, row - 2 * half, row)
    is_grad = of_role >= half
    in_half = jnp.where(is_grad, of_role - half, of_role)
    chosen = jnp.zeros(shape, jnp.float32)
    for mask in range(pieces):
        copy = in_half - jnp.bitwise_xor(own_slot, mask) * CAP
        wanted = copy + jnp.where(is_grad, CAP, 0) + jnp.where(is_second, 2 * CAP, 0) + mask * PIECE
        mine = jnp.logical_and(copy >= 0, copy < CAP)
        chosen = chosen + jnp.where(jnp.logical_and(mine, column == wanted), 1.0, 0.0)
    rows = jnp.concatenate([ref[...] for ref in ins], axis=0)
    both = dot(chosen.astype(jnp.bfloat16), rows, 1, 0)
    own_ref[...] = both[: 2 * half].astype(jnp.bfloat16)
    new_ref[...] = both[2 * half :].astype(jnp.bfloat16)


def join_pieces(arrays):
    pieces, width = len(arrays), arrays[0].shape[1]
    total = 2 * pieces * CAP
    tile = tile_of(width, 1792)
    return pl.pallas_call(
        functools.partial(join_kernel, pieces),
        grid=(width // tile,),
        in_specs=[pl.BlockSpec((PIECE, tile), lambda j: (0, j))] * pieces,
        out_specs=[pl.BlockSpec((total, tile), lambda j: (0, j))] * 2,
        out_shape=[jax.ShapeDtypeStruct((total, width), jnp.bfloat16)] * 2,
        compiler_params=params(),
        cost_estimate=cost(4 * total * PIECE * pieces * width, 8 * total * width),
        name="join_pieces",
    )(*arrays)


def rows_apart(refs, half, columns=None):
    blocks = [(ref, first) for ref in refs for first in range(0, ref.shape[0], 2 * half)]
    if columns is not None:
        blocks = [block for column in range(columns) for block in blocks[column::columns]]
    token_rows = jnp.concatenate([ref[first : first + half] for ref, first in blocks], axis=0)
    grad_rows = jnp.concatenate([ref[first + half : first + 2 * half] for ref, first in blocks], axis=0)
    return token_rows, grad_rows


def parts_spec(parts, tile):
    return [pl.BlockSpec((part.shape[0], tile), lambda j: (0, j)) for part in parts]


def factor_kernel(half, *refs):
    (w_in_ref, w_down_ref, out_ref, acc), x_refs = refs[-4:], refs[:-4]
    step = pl.program_id(0)
    units = w_down_ref.shape[1]

    @pl.when(step == 0)
    def _():
        acc[...] = jnp.zeros_like(acc)

    token_rows, grad_rows = rows_apart(x_refs, half)
    acc[0] += dot(token_rows, w_in_ref[0, 0], 1, 1)
    acc[1] += dot(token_rows, w_in_ref[0, 1], 1, 1)
    acc[2] += dot(grad_rows, w_down_ref[0], 1, 1)

    @pl.when(step == pl.num_programs(0) - 1)
    def _():
        gate, up, back = acc[0], acc[1], acc[2]
        sig = jax.nn.sigmoid(gate)
        activated = gate * sig
        slopes = sig * (1.0 + gate * (1.0 - sig))
        out_ref[:, 0:units] = (back * up * slopes).astype(jnp.bfloat16)
        out_ref[:, units : 2 * units] = (back * activated).astype(jnp.bfloat16)
        out_ref[:, 2 * units : 3 * units] = (activated * up).astype(jnp.bfloat16)


def factors_of(parts, w_in, w_down, half, weight):
    count, width = sum(part.shape[0] for part in parts) // 2, parts[0].shape[1]
    units = w_down.shape[1]
    tile = tile_of(width, 896)
    return pl.pallas_call(
        functools.partial(factor_kernel, half),
        grid=(width // tile,),
        in_specs=[
            *parts_spec(parts, tile),
            pl.BlockSpec((1, 2, units, tile), lambda j: (0, 0, 0, j)),
            pl.BlockSpec((1, units, tile), lambda j: (0, 0, j)),
        ],
        out_specs=pl.BlockSpec((count, 3 * units), lambda j: (0, 0)),
        out_shape=jax.ShapeDtypeStruct((count, 3 * units), jnp.bfloat16),
        scratch_shapes=[pltpu.VMEM((3, count, units), jnp.float32)],
        compiler_params=params(VMEM_LIMIT // 2),
        cost_estimate=cost(6 * weight * count * units * width, 6 * units * width + 4 * count * width),
        name="factors",
    )(*parts, w_in, w_down)


def pack_kernel(first, w_ref, one_ref, two_ref, out_ref):
    units = one_ref.shape[1]
    out_ref[: units - first] = w_ref[0, first:]
    out_ref[units - first : 2 * units - first] = one_ref[0].astype(jnp.bfloat16)
    out_ref[2 * units - first :] = two_ref[0].astype(jnp.bfloat16)


def pack(w_down, moment1, moment2, first):
    _, units, width = w_down.shape
    tile = tile_of(width, 896)
    spec = pl.BlockSpec((1, units, tile), lambda j: (0, 0, j))
    return pl.pallas_call(
        functools.partial(pack_kernel, first),
        grid=(width // tile,),
        in_specs=[spec, spec, spec],
        out_specs=pl.BlockSpec((3 * units - first, tile), lambda j: (0, j)),
        out_shape=jax.ShapeDtypeStruct((3 * units - first, width), jnp.bfloat16),
        compiler_params=params(),
        cost_estimate=cost(2 * units * width, 16 * units * width),
        name="pack_state",
    )(w_down, moment1, moment2)


def finish_kernel(half, columns, crossing, count, factor_ref, *refs):
    (down_ref, one_ref, two_ref, grad_ref, turned), x_refs = refs[-5:], refs[count:-5]
    units = down_ref.shape[1]

    @pl.when(pl.program_id(0) == 0)
    def _():
        turned[...] = factor_ref[...].astype(jnp.float32).T.astype(jnp.bfloat16)

    if crossing is None:
        token_rows, grad_rows = rows_apart(x_refs, half, columns)
    else:
        own_slot = lax.axis_index("expert")
        gathered = functools.reduce(jnp.logical_or, [own_slot == slot for slot in crossing])
        pairs = zip(rows_apart(x_refs[:-1], half), rows_apart(x_refs[-1:], half))
        token_rows, grad_rows = [jnp.where(gathered, theirs, mine) for theirs, mine in pairs]
    in_grads = dot(turned[: 2 * units], token_rows, 1, 0).astype(jnp.bfloat16)
    grad_ref[0, 0] = in_grads[:units]
    grad_ref[0, 1] = in_grads[units:]
    down_grad = dot(turned[2 * units :], grad_rows, 1, 0)
    rest = refs[count - 1]
    split = rest.shape[0] - 2 * units
    w_down = [refs[0][...], rest[:split]] if count == 2 else [rest[:split]]
    w_down = jnp.concatenate([part.astype(jnp.float32) for part in w_down], axis=0)
    moment1 = rest[split : split + units].astype(jnp.float32)
    moment2 = rest[split + units :].astype(jnp.float32)
    rate = adam_rate / (1.0 - beta_one**adam_step)
    fix_two = 1.0 / (1.0 - beta_two**adam_step)
    first_new = beta_one * moment1 + (1.0 - beta_one) * down_grad
    second_new = beta_two * moment2 + (1.0 - beta_two) * (down_grad * down_grad)
    change = rate * first_new / (jnp.sqrt(second_new * fix_two) + adam_eps)
    down_ref[0] = (w_down - change).astype(jnp.bfloat16)
    one_ref[0] = first_new
    two_ref[0] = second_new


def finish(factors, crossing, parts, states, half, columns):
    count, width = factors.shape[0], parts[0].shape[1]
    units = factors.shape[1] // 3
    tile = tile_of(width, 896)
    spec = pl.BlockSpec((1, units, tile), lambda j: (0, 0, j))
    kinds = (jnp.bfloat16, jnp.float32, jnp.float32)
    return pl.pallas_call(
        functools.partial(finish_kernel, half, columns, crossing, len(states)),
        grid=(width // tile,),
        in_specs=[
            pl.BlockSpec((count, 3 * units), lambda j: (0, 0)),
            *parts_spec(states, tile),
            *parts_spec(parts, tile),
        ],
        out_specs=[spec, spec, spec, pl.BlockSpec((1, 2, units, tile), lambda j: (0, 0, 0, j))],
        out_shape=[jax.ShapeDtypeStruct((1, units, width), kind) for kind in kinds]
        + [jax.ShapeDtypeStruct((1, 2, units, width), jnp.bfloat16)],
        scratch_shapes=[pltpu.VMEM((3 * units, count), jnp.bfloat16)],
        compiler_params=params(VMEM_LIMIT * 3 // 4),
        cost_estimate=cost(6 * count * units * width, 20 * units * width + 4 * count * width),
        name="finish",
    )(factors, *states, *parts)


def crossed(array, mask, slots=None):
    size = lax.axis_size("dp")
    if slots is None:
        return lax.ppermute(array, "dp", [(i, i ^ mask) for i in range(size)])
    pairs = [(s * size + i, s * size + (i ^ mask)) for s in slots for i in range(size)]
    return lax.ppermute(array, ("expert", "dp"), pairs)


def gather_own(block, columns, wait):
    planes = lax.axis_size("dp") // columns
    blocks = [block, crossed(block, columns)]
    for k in range(2, planes):
        blocks.append(crossed(block if k % 2 else after(block, blocks[1]), k * columns))
    near = jnp.concatenate(blocks[: planes // 2], axis=0)
    far = jnp.concatenate(blocks[planes // 2 :], axis=0)
    far = far if wait is None else after(far, wait)
    return [near, far] + [crossed(part, k) for k in range(1, columns) for part in (near, far)]


def gather_some(block, columns, slots):
    planes = lax.axis_size("dp") // columns
    blocks = [block] + [crossed(block, k * columns, slots) for k in range(1, planes)]
    plane = jnp.concatenate(blocks, axis=0)
    return [plane] + [crossed(plane, k, slots) for k in range(1, columns)]


def gather_half(block):
    held, mask = block, 1
    while 2 * mask < lax.axis_size("dp"):
        held = jnp.concatenate([held, crossed(held, mask)], axis=0)
        mask = 2 * mask
    return held


def after(array, *others):
    return lax.optimization_barrier((array, *others))[0]


def section_swaps(swap_code, slot, sections):
    swaps = []
    for bit in range(sections):
        lower = jnp.minimum(slot, jnp.bitwise_xor(slot, 1 << bit))
        swaps.append(swap_code[lower] // (1 << bit) % 2 == 1)
    return swaps


def static_order(expert_count, sections, swapped_pairs):
    order = list(range(expert_count))
    for bit in range(sections):
        step = [s ^ (1 << bit) if (bit, min(s, s ^ (1 << bit))) in swapped_pairs else s for s in range(expert_count)]
        order = [order[s] for s in step]
    return order


def layer(move, columns, order, operands):
    tokens, grad_out, route_weights, expert_ids, w_in, w_down, moment1, moment2 = operands
    expert_count = len(order)
    half = expert_count * CAP
    crossing = None
    if all(isinstance(slot, int) for slot in order):
        crossing = [s for s in range(expert_count) if order[s] not in (s, s ^ 1)]
    if crossing is not None and len(crossing) == expert_count:
        crossing = None

    picked = pick_rows(order, tokens, grad_out, route_weights, expert_ids)
    arrived = [picked[0]]
    for mask in range(1, expert_count):
        pairs = [(i, i ^ mask) for i in range(expert_count)]
        arrived.append(lax.ppermute(picked[mask], "expert", pairs))
    rows = max(16, w_down.shape[1] // 4) if crossing is None else 0
    packed = pack(after(w_down, picked[0]), moment1, moment2, rows)
    waits = arrived[1:]
    states = []
    if rows:
        states.append(move(w_down[0, :rows]))
        waits = waits + states
    states.append(move(after(packed, *waits) if rows else packed))
    if rows:
        arrived[0] = after(arrived[0], packed)
    own_block, new_block = join_pieces(arrived)
    if crossing is None:
        new_half = gather_half(new_block)
        own_parts = gather_own(own_block, columns, new_half)
        factors = factors_of(own_parts, w_in, w_down, half, 1)
        new_parts = [new_half, crossed(after(new_half, *own_parts[:3]), lax.axis_size("dp") // 2)]
    else:
        own_parts = gather_own(own_block, columns, None)
        factors = factors_of(own_parts, w_in, w_down, half, 40)
        new_parts = gather_some(after(new_block, *own_parts[:3]), columns, crossing)
        pairs = [(order[s], s) for s in range(expert_count) if s not in crossing]
        new_parts.append(lax.ppermute(after(jnp.concatenate(own_parts, axis=0), factors), "expert", pairs))
    factors = move(factors)
    return tuple(finish(factors, crossing, new_parts, states, half, columns))


def local(tokens, grad_out, route_weights, expert_ids, swap_code, w_in, w_down, moment1, moment2):
    expert_count = lax.axis_size("expert")
    sections = expert_count.bit_length() - 1
    columns = max(1, expert_count // 2)
    operands = (tokens, grad_out, route_weights, expert_ids, w_in, w_down, moment1, moment2)

    free = [(b, s) for b in range(sections) for s in range(1, expert_count) if not s >> b & 1]
    fixed = [(b, 0) for b in range(sections)]
    if len(free) <= 2:
        branches = []
        for taken in itertools.product((False, True), repeat=len(free)):
            pairs = fixed + [pair for pair, yes in zip(free, taken) if yes]
            order = static_order(expert_count, sections, pairs)
            move = functools.partial(
                lax.ppermute, axis_name="expert", perm=[(order[s], s) for s in range(expert_count)]
            )
            branches.append(functools.partial(layer, move, columns, order))
        which = jnp.int32(0)
        for bit, slot in free:
            which = which * 2 + ((swap_code[slot] >> bit) & 1)
        return lax.switch(which, branches, operands)

    swaps = section_swaps(swap_code, lax.axis_index("expert"), sections)

    def move_by_sections(array):
        for bit in range(sections):
            pairs = [(i, i ^ (1 << bit)) for i in range(expert_count)]
            array = jnp.where(swaps[bit], lax.ppermute(array, "expert", pairs), array)
        return array

    slots = jnp.arange(expert_count, dtype=jnp.int32)
    order = slots
    for bit in range(sections):
        partner = jnp.bitwise_xor(slots, 1 << bit)
        swapped = swap_code[jnp.minimum(slots, partner)] // (1 << bit) % 2 == 1
        order = order[jnp.where(swapped, partner, slots)]
    return layer(move_by_sections, columns, [order[s] for s in range(expert_count)], operands)


def solution(mesh):
    placed = (
        P(("expert", "dp"), None),
        P(("expert", "dp"), None),
        P(("expert", "dp"), None),
        P(("expert", "dp"), None),
        P(),
        P("expert", None, "dp", None),
        P("expert", "dp", None),
        P("expert", "dp", None),
        P("expert", "dp", None),
    )
    return jax.shard_map(
        local,
        mesh=mesh,
        in_specs=placed,
        out_specs=(
            P("expert", "dp", None),
            P("expert", "dp", None),
            P("expert", "dp", None),
            P("expert", None, "dp", None),
        ),
        check_vma=False,
    )
```

```python
import functools
import itertools

import jax
import jax.numpy as jnp
from jax import lax
from jax.experimental import pallas as pl
from jax.experimental.pallas import tpu as pltpu
from jax.sharding import PartitionSpec as P

CAP = 5
PIECE = 24
VMEM_LIMIT = 60 * 1024 * 1024

adam_rate = 0.01
beta_one = 0.9
beta_two = 0.999
adam_step = 100.0
adam_eps = 1e-08


def dot(left_side, right_side, left_dim, right_dim):
    return lax.dot_general(
        left_side,
        right_side,
        (((left_dim,), (right_dim,)), ((), ())),
        preferred_element_type=jnp.float32,
    )


def params(limit=VMEM_LIMIT):
    return pltpu.CompilerParams(vmem_limit_bytes=limit)


def cost(flops, nbytes):
    return pl.CostEstimate(flops=int(flops), bytes_accessed=int(nbytes), transcendentals=0)


def tile_of(width, most):
    tile = 128
    for count in range(1, width // 128 + 1):
        if width % (count * 128) == 0 and count * 128 <= most:
            tile = count * 128
    return tile


def pick_kernel(order, pieces, *refs):
    if order is None:
        order, refs = [refs[0][s] for s in range(pieces)], refs[1:]
    ids_ref, weights_ref, tok_ref, grad_ref = refs[:4]
    outs, (sel, scale) = refs[4 : 4 + pieces], refs[4 + pieces :]
    rows = tok_ref.shape[0]
    own_slot = lax.axis_index("expert")

    @pl.when(pl.program_id(0) == 0)
    def _():
        ids = ids_ref[...]
        weights = weights_ref[...]
        earlier = (
            lax.broadcasted_iota(jnp.int32, (rows, rows), 0)
            < lax.broadcasted_iota(jnp.int32, (rows, rows), 1)
        ).astype(jnp.bfloat16)
        want_count = 2 * pieces
        place = lax.broadcasted_iota(jnp.int32, (want_count, rows), 0)
        hits = jnp.zeros((want_count, rows), jnp.float32)
        shares = []
        for piece in range(pieces):
            slot = jnp.bitwise_xor(own_slot, piece)
            source = jnp.int32(0)
            for target in range(pieces):
                source = jnp.where(slot == target, order[target], source)
            for role, expert in enumerate((slot, source)):
                named = ids == expert
                hit = jnp.max(jnp.where(named, 1.0, 0.0), axis=0, keepdims=True)
                hits = jnp.where(place == 2 * piece + role, hit, hits)
                shares.append(jnp.sum(jnp.where(named, weights, 0.0), axis=0, keepdims=True))
        ranks = dot(hits.astype(jnp.bfloat16), earlier, 1, 0)
        ranks = jnp.where(hits > 0.0, ranks, -1.0).astype(jnp.int32)
        row = lax.broadcasted_iota(jnp.int32, (PIECE, rows), 0)
        of_role = jnp.where(row >= 2 * CAP, row - 2 * CAP, row)
        is_grad = of_role >= CAP
        copy = jnp.where(is_grad, of_role - CAP, of_role)
        for piece in range(pieces):
            first, second = 2 * piece, 2 * piece + 1
            is_first = row < 2 * CAP
            rank = jnp.where(is_first, ranks[first : first + 1], ranks[second : second + 1])
            share = jnp.where(is_first, shares[first], shares[second])
            match = jnp.logical_and(copy == rank, row < 4 * CAP)
            part = pl.ds(piece * PIECE, PIECE)
            sel[0, part] = jnp.where(jnp.logical_and(match, jnp.logical_not(is_grad)), 1.0, 0.0)
            sel[1, part] = jnp.where(jnp.logical_and(match, is_grad), 1.0, 0.0)
            scale[part] = jnp.sum(jnp.where(match, share, 0.0), axis=1, keepdims=True)

    token_part = dot(sel[0].astype(jnp.bfloat16), tok_ref[...], 1, 0)
    grad_part = dot(sel[1].astype(jnp.bfloat16), grad_ref[...], 1, 0)
    picked = token_part + scale[...] * grad_part
    for piece in range(pieces):
        outs[piece][...] = picked[piece * PIECE : (piece + 1) * PIECE].astype(jnp.bfloat16)


def pick_rows(order, tokens, grad_out, route_weights, expert_ids):
    pieces = len(order)
    rows, width = tokens.shape
    top = expert_ids.shape[1]
    total = pieces * PIECE
    tile = tile_of(width, 1792)
    known = all(isinstance(s, int) for s in order)
    return pl.pallas_call(
        functools.partial(pick_kernel, tuple(order) if known else None, pieces),
        grid_spec=pltpu.PrefetchScalarGridSpec(
            num_scalar_prefetch=0 if known else 1,
            grid=(width // tile,),
            in_specs=[
                pl.BlockSpec((top, rows), lambda j, *_: (0, 0)),
                pl.BlockSpec((top, rows), lambda j, *_: (0, 0)),
                pl.BlockSpec((rows, tile), lambda j, *_: (0, j)),
                pl.BlockSpec((rows, tile), lambda j, *_: (0, j)),
            ],
            out_specs=[pl.BlockSpec((PIECE, tile), lambda j, *_: (0, j))] * pieces,
            scratch_shapes=[
                pltpu.VMEM((2, total, rows), jnp.float32),
                pltpu.VMEM((total, 1), jnp.float32),
            ],
        ),
        out_shape=[jax.ShapeDtypeStruct((PIECE, width), jnp.bfloat16)] * pieces,
        compiler_params=params(),
        cost_estimate=cost(4 * total * rows * width, 4 * rows * width),
        name="pick_rows",
    )(*(() if known else (jnp.stack(order),)), expert_ids.T, route_weights.T, tokens, grad_out)


def join_kernel(pieces, *refs):
    ins, (own_ref, new_ref) = refs[:pieces], refs[pieces:]
    half = pieces * CAP
    own_slot = lax.axis_index("expert")
    shape = (4 * half, pieces * PIECE)
    row = lax.broadcasted_iota(jnp.int32, shape, 0)
    column = lax.broadcasted_iota(jnp.int32, shape, 1)
    is_second = row >= 2 * half
    of_role = jnp.where(is_second, row - 2 * half, row)
    is_grad = of_role >= half
    in_half = jnp.where(is_grad, of_role - half, of_role)
    chosen = jnp.zeros(shape, jnp.float32)
    for mask in range(pieces):
        copy = in_half - jnp.bitwise_xor(own_slot, mask) * CAP
        wanted = copy + jnp.where(is_grad, CAP, 0) + jnp.where(is_second, 2 * CAP, 0) + mask * PIECE
        mine = jnp.logical_and(copy >= 0, copy < CAP)
        chosen = chosen + jnp.where(jnp.logical_and(mine, column == wanted), 1.0, 0.0)
    rows = jnp.concatenate([ref[...] for ref in ins], axis=0)
    both = dot(chosen.astype(jnp.bfloat16), rows, 1, 0)
    own_ref[...] = both[: 2 * half].astype(jnp.bfloat16)
    new_ref[...] = both[2 * half :].astype(jnp.bfloat16)


def join_pieces(arrays):
    pieces, width = len(arrays), arrays[0].shape[1]
    total = 2 * pieces * CAP
    tile = tile_of(width, 1792)
    return pl.pallas_call(
        functools.partial(join_kernel, pieces),
        grid=(width // tile,),
        in_specs=[pl.BlockSpec((PIECE, tile), lambda j: (0, j))] * pieces,
        out_specs=[pl.BlockSpec((total, tile), lambda j: (0, j))] * 2,
        out_shape=[jax.ShapeDtypeStruct((total, width), jnp.bfloat16)] * 2,
        compiler_params=params(),
        cost_estimate=cost(4 * total * PIECE * pieces * width, 8 * total * width),
        name="join_pieces",
    )(*arrays)


def rows_apart(refs, half, columns=None):
    blocks = [(ref, first) for ref in refs for first in range(0, ref.shape[0], 2 * half)]
    if columns is not None:
        blocks = [block for column in range(columns) for block in blocks[column::columns]]
    token_rows = jnp.concatenate([ref[first : first + half] for ref, first in blocks], axis=0)
    grad_rows = jnp.concatenate([ref[first + half : first + 2 * half] for ref, first in blocks], axis=0)
    return token_rows, grad_rows


def parts_spec(parts, tile):
    return [pl.BlockSpec((part.shape[0], tile), lambda j: (0, j)) for part in parts]


def factor_kernel(half, *refs):
    (w_in_ref, w_down_ref, out_ref, acc), x_refs = refs[-4:], refs[:-4]
    step = pl.program_id(0)
    units = w_down_ref.shape[1]

    @pl.when(step == 0)
    def _():
        acc[...] = jnp.zeros_like(acc)

    token_rows, grad_rows = rows_apart(x_refs, half)
    acc[0] += dot(token_rows, w_in_ref[0, 0], 1, 1)
    acc[1] += dot(token_rows, w_in_ref[0, 1], 1, 1)
    acc[2] += dot(grad_rows, w_down_ref[0], 1, 1)

    @pl.when(step == pl.num_programs(0) - 1)
    def _():
        gate, up, back = acc[0], acc[1], acc[2]
        sig = jax.nn.sigmoid(gate)
        activated = gate * sig
        slopes = sig * (1.0 + gate * (1.0 - sig))
        out_ref[:, 0:units] = (back * up * slopes).astype(jnp.bfloat16)
        out_ref[:, units : 2 * units] = (back * activated).astype(jnp.bfloat16)
        out_ref[:, 2 * units : 3 * units] = (activated * up).astype(jnp.bfloat16)


def factors_of(parts, w_in, w_down, half, weight):
    count, width = sum(part.shape[0] for part in parts) // 2, parts[0].shape[1]
    units = w_down.shape[1]
    tile = tile_of(width, 896)
    return pl.pallas_call(
        functools.partial(factor_kernel, half),
        grid=(width // tile,),
        in_specs=[
            *parts_spec(parts, tile),
            pl.BlockSpec((1, 2, units, tile), lambda j: (0, 0, 0, j)),
            pl.BlockSpec((1, units, tile), lambda j: (0, 0, j)),
        ],
        out_specs=pl.BlockSpec((count, 3 * units), lambda j: (0, 0)),
        out_shape=jax.ShapeDtypeStruct((count, 3 * units), jnp.bfloat16),
        scratch_shapes=[pltpu.VMEM((3, count, units), jnp.float32)],
        compiler_params=params(VMEM_LIMIT // 2),
        cost_estimate=cost(6 * weight * count * units * width, 6 * units * width + 4 * count * width),
        name="factors",
    )(*parts, w_in, w_down)


def pack_kernel(first, w_ref, one_ref, two_ref, out_ref):
    units = one_ref.shape[1]
    out_ref[: units - first] = w_ref[0, first:]
    out_ref[units - first : 2 * units - first] = one_ref[0].astype(jnp.bfloat16)
    out_ref[2 * units - first :] = two_ref[0].astype(jnp.bfloat16)


def pack(w_down, moment1, moment2, first):
    _, units, width = w_down.shape
    tile = tile_of(width, 896)
    spec = pl.BlockSpec((1, units, tile), lambda j: (0, 0, j))
    return pl.pallas_call(
        functools.partial(pack_kernel, first),
        grid=(width // tile,),
        in_specs=[spec, spec, spec],
        out_specs=pl.BlockSpec((3 * units - first, tile), lambda j: (0, j)),
        out_shape=jax.ShapeDtypeStruct((3 * units - first, width), jnp.bfloat16),
        compiler_params=params(),
        cost_estimate=cost(2 * units * width, 16 * units * width),
        name="pack_state",
    )(w_down, moment1, moment2)


def finish_kernel(half, columns, crossing, count, factor_ref, *refs):
    (down_ref, one_ref, two_ref, grad_ref, turned), x_refs = refs[-5:], refs[count:-5]
    units = down_ref.shape[1]

    @pl.when(pl.program_id(0) == 0)
    def _():
        turned[...] = factor_ref[...].astype(jnp.float32).T.astype(jnp.bfloat16)

    if crossing is None:
        token_rows, grad_rows = rows_apart(x_refs, half, columns)
    else:
        own_slot = lax.axis_index("expert")
        gathered = functools.reduce(jnp.logical_or, [own_slot == slot for slot in crossing])
        pairs = zip(rows_apart(x_refs[:-1], half), rows_apart(x_refs[-1:], half))
        token_rows, grad_rows = [jnp.where(gathered, theirs, mine) for theirs, mine in pairs]
    in_grads = dot(turned[: 2 * units], token_rows, 1, 0).astype(jnp.bfloat16)
    grad_ref[0, 0] = in_grads[:units]
    grad_ref[0, 1] = in_grads[units:]
    down_grad = dot(turned[2 * units :], grad_rows, 1, 0)
    rest = refs[count - 1]
    split = rest.shape[0] - 2 * units
    w_down = [refs[0][...], rest[:split]] if count == 2 else [rest[:split]]
    w_down = jnp.concatenate([part.astype(jnp.float32) for part in w_down], axis=0)
    moment1 = rest[split : split + units].astype(jnp.float32)
    moment2 = rest[split + units :].astype(jnp.float32)
    rate = adam_rate / (1.0 - beta_one**adam_step)
    fix_two = 1.0 / (1.0 - beta_two**adam_step)
    first_new = beta_one * moment1 + (1.0 - beta_one) * down_grad
    second_new = beta_two * moment2 + (1.0 - beta_two) * (down_grad * down_grad)
    change = rate * first_new / (jnp.sqrt(second_new * fix_two) + adam_eps)
    down_ref[0] = (w_down - change).astype(jnp.bfloat16)
    one_ref[0] = first_new
    two_ref[0] = second_new


def finish(factors, crossing, parts, states, half, columns):
    count, width = factors.shape[0], parts[0].shape[1]
    units = factors.shape[1] // 3
    tile = tile_of(width, 896)
    spec = pl.BlockSpec((1, units, tile), lambda j: (0, 0, j))
    kinds = (jnp.bfloat16, jnp.float32, jnp.float32)
    return pl.pallas_call(
        functools.partial(finish_kernel, half, columns, crossing, len(states)),
        grid=(width // tile,),
        in_specs=[
            pl.BlockSpec((count, 3 * units), lambda j: (0, 0)),
            *parts_spec(states, tile),
            *parts_spec(parts, tile),
        ],
        out_specs=[spec, spec, spec, pl.BlockSpec((1, 2, units, tile), lambda j: (0, 0, 0, j))],
        out_shape=[jax.ShapeDtypeStruct((1, units, width), kind) for kind in kinds]
        + [jax.ShapeDtypeStruct((1, 2, units, width), jnp.bfloat16)],
        scratch_shapes=[pltpu.VMEM((3 * units, count), jnp.bfloat16)],
        compiler_params=params(VMEM_LIMIT * 3 // 4),
        cost_estimate=cost(6 * count * units * width, 20 * units * width + 4 * count * width),
        name="finish",
    )(factors, *states, *parts)


def crossed(array, mask, slots=None):
    size = lax.axis_size("dp")
    if slots is None:
        return lax.ppermute(array, "dp", [(i, i ^ mask) for i in range(size)])
    pairs = [(s * size + i, s * size + (i ^ mask)) for s in slots for i in range(size)]
    return lax.ppermute(array, ("expert", "dp"), pairs)


def gather_own(block, columns, wait):
    planes = lax.axis_size("dp") // columns
    blocks = [block, crossed(block, columns)]
    for k in range(2, planes):
        blocks.append(crossed(block if k % 2 else after(block, blocks[1]), k * columns))
    near = jnp.concatenate(blocks[: planes // 2], axis=0)
    far = jnp.concatenate(blocks[planes // 2 :], axis=0)
    far = far if wait is None else after(far, wait)
    return [near, far] + [crossed(part, k) for k in range(1, columns) for part in (near, far)]


def gather_some(block, columns, slots):
    planes = lax.axis_size("dp") // columns
    blocks = [crossed(block, k * columns, slots) for k in reversed(range(1, planes))]
    blocks = [block] + blocks[::-1]
    near = jnp.concatenate(blocks[: planes // 2], axis=0)
    far = jnp.concatenate(blocks[planes // 2 :], axis=0)
    return [near, far] + [crossed(part, k, slots) for k in range(1, columns) for part in (near, far)]


def gather_half(block):
    held, mask = block, 1
    while 2 * mask < lax.axis_size("dp"):
        held = jnp.concatenate([held, crossed(held, mask)], axis=0)
        mask = 2 * mask
    return held


def after(array, *others):
    return lax.optimization_barrier((array, *others))[0]


def section_swaps(swap_code, slot, sections):
    swaps = []
    for bit in range(sections):
        lower = jnp.minimum(slot, jnp.bitwise_xor(slot, 1 << bit))
        swaps.append(swap_code[lower] // (1 << bit) % 2 == 1)
    return swaps


def static_order(expert_count, sections, swapped_pairs):
    order = list(range(expert_count))
    for bit in range(sections):
        step = [s ^ (1 << bit) if (bit, min(s, s ^ (1 << bit))) in swapped_pairs else s for s in range(expert_count)]
        order = [order[s] for s in step]
    return order


def layer(move, columns, order, operands):
    tokens, grad_out, route_weights, expert_ids, w_in, w_down, moment1, moment2 = operands
    expert_count = len(order)
    half = expert_count * CAP
    crossing = None
    if all(isinstance(slot, int) for slot in order):
        crossing = [s for s in range(expert_count) if order[s] not in (s, s ^ 1)]
    if crossing is not None and len(crossing) == expert_count:
        crossing = None

    picked = pick_rows(order, tokens, grad_out, route_weights, expert_ids)
    arrived = [picked[0]]
    for mask in range(1, expert_count):
        pairs = [(i, i ^ mask) for i in range(expert_count)]
        arrived.append(lax.ppermute(picked[mask], "expert", pairs))
    rows = max(16, w_down.shape[1] // 4) if crossing is None else 0
    packed = pack(after(w_down, picked[0]), moment1, moment2, rows)
    waits = arrived[1:]
    states = []
    if rows:
        states.append(move(w_down[0, :rows]))
        waits = waits + states
    states.append(move(after(packed, *waits)))
    arrived[0] = after(arrived[0], packed)
    own_block, new_block = join_pieces(arrived)
    if crossing is None:
        new_half = gather_half(new_block)
        own_parts = gather_own(own_block, columns, new_half)
        factors = factors_of(own_parts, w_in, w_down, half, 1)
        new_parts = [new_half, crossed(after(new_half, *own_parts[:3]), lax.axis_size("dp") // 2)]
    else:
        own_parts = gather_own(own_block, columns, None)
        factors = factors_of(own_parts, w_in, w_down, half, 12)
        new_parts = gather_some(after(new_block, *own_parts[:3]), columns, crossing)
        pairs = [(order[s], s) for s in range(expert_count) if s not in crossing]
        new_parts.append(lax.ppermute(after(jnp.concatenate(own_parts, axis=0), factors), "expert", pairs))
    factors = move(factors)
    return tuple(finish(factors, crossing, new_parts, states, half, columns))


def local(tokens, grad_out, route_weights, expert_ids, swap_code, w_in, w_down, moment1, moment2):
    expert_count = lax.axis_size("expert")
    sections = expert_count.bit_length() - 1
    columns = max(1, expert_count // 2)
    operands = (tokens, grad_out, route_weights, expert_ids, w_in, w_down, moment1, moment2)

    free = [(b, s) for b in range(sections) for s in range(1, expert_count) if not s >> b & 1]
    fixed = [(b, 0) for b in range(sections)]
    if len(free) <= 2:
        branches = []
        for taken in itertools.product((False, True), repeat=len(free)):
            pairs = fixed + [pair for pair, yes in zip(free, taken) if yes]
            order = static_order(expert_count, sections, pairs)
            move = functools.partial(
                lax.ppermute, axis_name="expert", perm=[(order[s], s) for s in range(expert_count)]
            )
            branches.append(functools.partial(layer, move, columns, order))
        which = jnp.int32(0)
        for bit, slot in free:
            which = which * 2 + ((swap_code[slot] >> bit) & 1)
        return lax.switch(which, branches, operands)

    swaps = section_swaps(swap_code, lax.axis_index("expert"), sections)

    def move_by_sections(array):
        for bit in range(sections):
            pairs = [(i, i ^ (1 << bit)) for i in range(expert_count)]
            array = jnp.where(swaps[bit], lax.ppermute(array, "expert", pairs), array)
        return array

    slots = jnp.arange(expert_count, dtype=jnp.int32)
    order = slots
    for bit in range(sections):
        partner = jnp.bitwise_xor(slots, 1 << bit)
        swapped = swap_code[jnp.minimum(slots, partner)] // (1 << bit) % 2 == 1
        order = order[jnp.where(swapped, partner, slots)]
    return layer(move_by_sections, columns, [order[s] for s in range(expert_count)], operands)


def solution(mesh):
    placed = (
        P(("expert", "dp"), None),
        P(("expert", "dp"), None),
        P(("expert", "dp"), None),
        P(("expert", "dp"), None),
        P(),
        P("expert", None, "dp", None),
        P("expert", "dp", None),
        P("expert", "dp", None),
        P("expert", "dp", None),
    )
    return jax.shard_map(
        local,
        mesh=mesh,
        in_specs=placed,
        out_specs=(
            P("expert", "dp", None),
            P("expert", "dp", None),
            P("expert", "dp", None),
            P("expert", None, "dp", None),
        ),
        check_vma=False,
    )
```

```python
import functools
import itertools

import jax
import jax.numpy as jnp
from jax import lax
from jax.experimental import pallas as pl
from jax.experimental.pallas import tpu as pltpu
from jax.sharding import PartitionSpec as P

CAP = 5
PIECE = 24
VMEM_LIMIT = 60 * 1024 * 1024

adam_rate = 0.01
beta_one = 0.9
beta_two = 0.999
adam_step = 100.0
adam_eps = 1e-08


def dot(left_side, right_side, left_dim, right_dim):
    return lax.dot_general(
        left_side,
        right_side,
        (((left_dim,), (right_dim,)), ((), ())),
        preferred_element_type=jnp.float32,
    )


def params(limit=VMEM_LIMIT):
    return pltpu.CompilerParams(vmem_limit_bytes=limit)


def cost(flops, nbytes):
    return pl.CostEstimate(flops=int(flops), bytes_accessed=int(nbytes), transcendentals=0)


def tile_of(width, most):
    tile = 128
    for count in range(1, width // 128 + 1):
        if width % (count * 128) == 0 and count * 128 <= most:
            tile = count * 128
    return tile


def pick_kernel(order, pieces, *refs):
    if order is None:
        order, refs = [refs[0][s] for s in range(pieces)], refs[1:]
    ids_ref, weights_ref, tok_ref, grad_ref = refs[:4]
    outs, (sel, scale) = refs[4 : 4 + pieces], refs[4 + pieces :]
    rows = tok_ref.shape[0]
    own_slot = lax.axis_index("expert")

    @pl.when(pl.program_id(0) == 0)
    def _():
        ids = ids_ref[...]
        weights = weights_ref[...]
        earlier = (
            lax.broadcasted_iota(jnp.int32, (rows, rows), 0)
            < lax.broadcasted_iota(jnp.int32, (rows, rows), 1)
        ).astype(jnp.bfloat16)
        want_count = 2 * pieces
        place = lax.broadcasted_iota(jnp.int32, (want_count, rows), 0)
        hits = jnp.zeros((want_count, rows), jnp.float32)
        shares = []
        for piece in range(pieces):
            slot = jnp.bitwise_xor(own_slot, piece)
            source = jnp.int32(0)
            for target in range(pieces):
                source = jnp.where(slot == target, order[target], source)
            for role, expert in enumerate((slot, source)):
                named = ids == expert
                hit = jnp.max(jnp.where(named, 1.0, 0.0), axis=0, keepdims=True)
                hits = jnp.where(place == 2 * piece + role, hit, hits)
                shares.append(jnp.sum(jnp.where(named, weights, 0.0), axis=0, keepdims=True))
        ranks = dot(hits.astype(jnp.bfloat16), earlier, 1, 0)
        ranks = jnp.where(hits > 0.0, ranks, -1.0).astype(jnp.int32)
        row = lax.broadcasted_iota(jnp.int32, (PIECE, rows), 0)
        of_role = jnp.where(row >= 2 * CAP, row - 2 * CAP, row)
        is_grad = of_role >= CAP
        copy = jnp.where(is_grad, of_role - CAP, of_role)
        for piece in range(pieces):
            first, second = 2 * piece, 2 * piece + 1
            is_first = row < 2 * CAP
            rank = jnp.where(is_first, ranks[first : first + 1], ranks[second : second + 1])
            share = jnp.where(is_first, shares[first], shares[second])
            match = jnp.logical_and(copy == rank, row < 4 * CAP)
            part = pl.ds(piece * PIECE, PIECE)
            sel[0, part] = jnp.where(jnp.logical_and(match, jnp.logical_not(is_grad)), 1.0, 0.0)
            sel[1, part] = jnp.where(jnp.logical_and(match, is_grad), 1.0, 0.0)
            scale[part] = jnp.sum(jnp.where(match, share, 0.0), axis=1, keepdims=True)

    token_part = dot(sel[0].astype(jnp.bfloat16), tok_ref[...], 1, 0)
    grad_part = dot(sel[1].astype(jnp.bfloat16), grad_ref[...], 1, 0)
    picked = token_part + scale[...] * grad_part
    for piece in range(pieces):
        outs[piece][...] = picked[piece * PIECE : (piece + 1) * PIECE].astype(jnp.bfloat16)


def pick_rows(order, tokens, grad_out, route_weights, expert_ids):
    pieces = len(order)
    rows, width = tokens.shape
    top = expert_ids.shape[1]
    total = pieces * PIECE
    tile = tile_of(width, 1792)
    known = all(isinstance(s, int) for s in order)
    return pl.pallas_call(
        functools.partial(pick_kernel, tuple(order) if known else None, pieces),
        grid_spec=pltpu.PrefetchScalarGridSpec(
            num_scalar_prefetch=0 if known else 1,
            grid=(width // tile,),
            in_specs=[
                pl.BlockSpec((top, rows), lambda j, *_: (0, 0)),
                pl.BlockSpec((top, rows), lambda j, *_: (0, 0)),
                pl.BlockSpec((rows, tile), lambda j, *_: (0, j)),
                pl.BlockSpec((rows, tile), lambda j, *_: (0, j)),
            ],
            out_specs=[pl.BlockSpec((PIECE, tile), lambda j, *_: (0, j))] * pieces,
            scratch_shapes=[
                pltpu.VMEM((2, total, rows), jnp.float32),
                pltpu.VMEM((total, 1), jnp.float32),
            ],
        ),
        out_shape=[jax.ShapeDtypeStruct((PIECE, width), jnp.bfloat16)] * pieces,
        compiler_params=params(),
        cost_estimate=cost(4 * total * rows * width, 4 * rows * width),
        name="pick_rows",
    )(*(() if known else (jnp.stack(order),)), expert_ids.T, route_weights.T, tokens, grad_out)


def join_kernel(pieces, *refs):
    ins, (own_ref, new_ref) = refs[:pieces], refs[pieces:]
    half = pieces * CAP
    own_slot = lax.axis_index("expert")
    shape = (4 * half, pieces * PIECE)
    row = lax.broadcasted_iota(jnp.int32, shape, 0)
    column = lax.broadcasted_iota(jnp.int32, shape, 1)
    is_second = row >= 2 * half
    of_role = jnp.where(is_second, row - 2 * half, row)
    is_grad = of_role >= half
    in_half = jnp.where(is_grad, of_role - half, of_role)
    chosen = jnp.zeros(shape, jnp.float32)
    for mask in range(pieces):
        copy = in_half - jnp.bitwise_xor(own_slot, mask) * CAP
        wanted = copy + jnp.where(is_grad, CAP, 0) + jnp.where(is_second, 2 * CAP, 0) + mask * PIECE
        mine = jnp.logical_and(copy >= 0, copy < CAP)
        chosen = chosen + jnp.where(jnp.logical_and(mine, column == wanted), 1.0, 0.0)
    rows = jnp.concatenate([ref[...] for ref in ins], axis=0)
    both = dot(chosen.astype(jnp.bfloat16), rows, 1, 0)
    own_ref[...] = both[: 2 * half].astype(jnp.bfloat16)
    new_ref[...] = both[2 * half :].astype(jnp.bfloat16)


def join_pieces(arrays):
    pieces, width = len(arrays), arrays[0].shape[1]
    total = 2 * pieces * CAP
    tile = tile_of(width, 1792)
    return pl.pallas_call(
        functools.partial(join_kernel, pieces),
        grid=(width // tile,),
        in_specs=[pl.BlockSpec((PIECE, tile), lambda j: (0, j))] * pieces,
        out_specs=[pl.BlockSpec((total, tile), lambda j: (0, j))] * 2,
        out_shape=[jax.ShapeDtypeStruct((total, width), jnp.bfloat16)] * 2,
        compiler_params=params(),
        cost_estimate=cost(4 * total * PIECE * pieces * width, 8 * total * width),
        name="join_pieces",
    )(*arrays)


def rows_apart(refs, half, columns=None):
    blocks = [(ref, first) for ref in refs for first in range(0, ref.shape[0], 2 * half)]
    if columns is not None:
        blocks = [block for column in range(columns) for block in blocks[column::columns]]
    token_rows = jnp.concatenate([ref[first : first + half] for ref, first in blocks], axis=0)
    grad_rows = jnp.concatenate([ref[first + half : first + 2 * half] for ref, first in blocks], axis=0)
    return token_rows, grad_rows


def parts_spec(parts, tile):
    return [pl.BlockSpec((part.shape[0], tile), lambda j: (0, j)) for part in parts]


def factor_kernel(half, *refs):
    (w_in_ref, w_down_ref, out_ref, acc), x_refs = refs[-4:], refs[:-4]
    step = pl.program_id(0)
    units = w_down_ref.shape[1]

    @pl.when(step == 0)
    def _():
        acc[...] = jnp.zeros_like(acc)

    token_rows, grad_rows = rows_apart(x_refs, half)
    acc[0] += dot(token_rows, w_in_ref[0, 0], 1, 1)
    acc[1] += dot(token_rows, w_in_ref[0, 1], 1, 1)
    acc[2] += dot(grad_rows, w_down_ref[0], 1, 1)

    @pl.when(step == pl.num_programs(0) - 1)
    def _():
        gate, up, back = acc[0], acc[1], acc[2]
        sig = jax.nn.sigmoid(gate)
        activated = gate * sig
        slopes = sig * (1.0 + gate * (1.0 - sig))
        out_ref[:, 0:units] = (back * up * slopes).astype(jnp.bfloat16)
        out_ref[:, units : 2 * units] = (back * activated).astype(jnp.bfloat16)
        out_ref[:, 2 * units : 3 * units] = (activated * up).astype(jnp.bfloat16)


def factors_of(parts, w_in, w_down, half, weight):
    count, width = sum(part.shape[0] for part in parts) // 2, parts[0].shape[1]
    units = w_down.shape[1]
    tile = tile_of(width, 896)
    return pl.pallas_call(
        functools.partial(factor_kernel, half),
        grid=(width // tile,),
        in_specs=[
            *parts_spec(parts, tile),
            pl.BlockSpec((1, 2, units, tile), lambda j: (0, 0, 0, j)),
            pl.BlockSpec((1, units, tile), lambda j: (0, 0, j)),
        ],
        out_specs=pl.BlockSpec((count, 3 * units), lambda j: (0, 0)),
        out_shape=jax.ShapeDtypeStruct((count, 3 * units), jnp.bfloat16),
        scratch_shapes=[pltpu.VMEM((3, count, units), jnp.float32)],
        compiler_params=params(VMEM_LIMIT // 2),
        cost_estimate=cost(6 * weight * count * units * width, 6 * units * width + 4 * count * width),
        name="factors",
    )(*parts, w_in, w_down)


def pack_kernel(first, w_ref, one_ref, two_ref, out_ref):
    units = one_ref.shape[1]
    out_ref[: units - first] = w_ref[0, first:]
    out_ref[units - first : 2 * units - first] = one_ref[0].astype(jnp.bfloat16)
    out_ref[2 * units - first :] = two_ref[0].astype(jnp.bfloat16)


def pack(w_down, moment1, moment2, first):
    _, units, width = w_down.shape
    tile = tile_of(width, 896)
    spec = pl.BlockSpec((1, units, tile), lambda j: (0, 0, j))
    return pl.pallas_call(
        functools.partial(pack_kernel, first),
        grid=(width // tile,),
        in_specs=[spec, spec, spec],
        out_specs=pl.BlockSpec((3 * units - first, tile), lambda j: (0, j)),
        out_shape=jax.ShapeDtypeStruct((3 * units - first, width), jnp.bfloat16),
        compiler_params=params(),
        cost_estimate=cost(2 * units * width, 16 * units * width),
        name="pack_state",
    )(w_down, moment1, moment2)


def finish_kernel(half, columns, crossing, count, factor_ref, *refs):
    (down_ref, one_ref, two_ref, grad_ref, turned), x_refs = refs[-5:], refs[count:-5]
    units = down_ref.shape[1]

    @pl.when(pl.program_id(0) == 0)
    def _():
        turned[...] = factor_ref[...].astype(jnp.float32).T.astype(jnp.bfloat16)

    if crossing is None:
        token_rows, grad_rows = rows_apart(x_refs, half, columns)
    else:
        own_slot = lax.axis_index("expert")
        gathered = functools.reduce(jnp.logical_or, [own_slot == slot for slot in crossing])
        pairs = zip(rows_apart(x_refs[:-1], half), rows_apart(x_refs[-1:], half))
        token_rows, grad_rows = [jnp.where(gathered, theirs, mine) for theirs, mine in pairs]
    in_grads = dot(turned[: 2 * units], token_rows, 1, 0).astype(jnp.bfloat16)
    grad_ref[0, 0] = in_grads[:units]
    grad_ref[0, 1] = in_grads[units:]
    down_grad = dot(turned[2 * units :], grad_rows, 1, 0)
    rest = refs[count - 1]
    split = rest.shape[0] - 2 * units
    w_down = [refs[0][...], rest[:split]] if count == 2 else [rest[:split]]
    w_down = jnp.concatenate([part.astype(jnp.float32) for part in w_down], axis=0)
    moment1 = rest[split : split + units].astype(jnp.float32)
    moment2 = rest[split + units :].astype(jnp.float32)
    rate = adam_rate / (1.0 - beta_one**adam_step)
    fix_two = 1.0 / (1.0 - beta_two**adam_step)
    first_new = beta_one * moment1 + (1.0 - beta_one) * down_grad
    second_new = beta_two * moment2 + (1.0 - beta_two) * (down_grad * down_grad)
    change = rate * first_new / (jnp.sqrt(second_new * fix_two) + adam_eps)
    down_ref[0] = (w_down - change).astype(jnp.bfloat16)
    one_ref[0] = first_new
    two_ref[0] = second_new


def finish(factors, crossing, parts, states, half, columns):
    count, width = factors.shape[0], parts[0].shape[1]
    units = factors.shape[1] // 3
    tile = tile_of(width, 896)
    spec = pl.BlockSpec((1, units, tile), lambda j: (0, 0, j))
    kinds = (jnp.bfloat16, jnp.float32, jnp.float32)
    return pl.pallas_call(
        functools.partial(finish_kernel, half, columns, crossing, len(states)),
        grid=(width // tile,),
        in_specs=[
            pl.BlockSpec((count, 3 * units), lambda j: (0, 0)),
            *parts_spec(states, tile),
            *parts_spec(parts, tile),
        ],
        out_specs=[spec, spec, spec, pl.BlockSpec((1, 2, units, tile), lambda j: (0, 0, 0, j))],
        out_shape=[jax.ShapeDtypeStruct((1, units, width), kind) for kind in kinds]
        + [jax.ShapeDtypeStruct((1, 2, units, width), jnp.bfloat16)],
        scratch_shapes=[pltpu.VMEM((3 * units, count), jnp.bfloat16)],
        compiler_params=params(VMEM_LIMIT // 2),
        cost_estimate=cost(6 * count * units * width, 20 * units * width + 4 * count * width),
        name="finish",
    )(factors, *states, *parts)


def crossed(array, mask, slots=None):
    size = lax.axis_size("dp")
    if slots is None:
        return lax.ppermute(array, "dp", [(i, i ^ mask) for i in range(size)])
    pairs = [(s * size + i, s * size + (i ^ mask)) for s in slots for i in range(size)]
    return lax.ppermute(array, ("expert", "dp"), pairs)


def gather_own(block, columns, wait):
    planes = lax.axis_size("dp") // columns
    blocks = [block, crossed(block, columns)]
    for k in range(2, planes):
        blocks.append(crossed(block if k % 2 else after(block, blocks[1]), k * columns))
    near = jnp.concatenate(blocks[: planes // 2], axis=0)
    far = jnp.concatenate(blocks[planes // 2 :], axis=0)
    far = far if wait is None else after(far, wait)
    return [near, far] + [crossed(part, k) for k in range(1, columns) for part in (near, far)]


def gather_some(block, columns, slots):
    planes = lax.axis_size("dp") // columns
    blocks = [crossed(block, k * columns, slots) for k in reversed(range(1, planes))]
    blocks = [block] + blocks[::-1]
    near = jnp.concatenate(blocks[: planes // 2], axis=0)
    far = jnp.concatenate(blocks[planes // 2 :], axis=0)
    return [near, far] + [crossed(part, k, slots) for k in range(1, columns) for part in (near, far)]


def gather_half(block):
    held, mask = block, 1
    while 2 * mask < lax.axis_size("dp"):
        held = jnp.concatenate([held, crossed(held, mask)], axis=0)
        mask = 2 * mask
    return held


def after(array, *others):
    return lax.optimization_barrier((array, *others))[0]


def section_swaps(swap_code, slot, sections):
    swaps = []
    for bit in range(sections):
        lower = jnp.minimum(slot, jnp.bitwise_xor(slot, 1 << bit))
        swaps.append(swap_code[lower] // (1 << bit) % 2 == 1)
    return swaps


def static_order(expert_count, sections, swapped_pairs):
    order = list(range(expert_count))
    for bit in range(sections):
        step = [s ^ (1 << bit) if (bit, min(s, s ^ (1 << bit))) in swapped_pairs else s for s in range(expert_count)]
        order = [order[s] for s in step]
    return order


def layer(move, columns, order, operands):
    tokens, grad_out, route_weights, expert_ids, w_in, w_down, moment1, moment2 = operands
    expert_count = len(order)
    half = expert_count * CAP
    crossing = None
    if all(isinstance(slot, int) for slot in order):
        crossing = [s for s in range(expert_count) if order[s] not in (s, s ^ 1)]
    if crossing is not None and len(crossing) == expert_count:
        crossing = None

    picked = pick_rows(order, tokens, grad_out, route_weights, expert_ids)
    arrived = [picked[0]]
    for mask in range(1, expert_count):
        pairs = [(i, i ^ mask) for i in range(expert_count)]
        arrived.append(lax.ppermute(picked[mask], "expert", pairs))
    rows = max(16, w_down.shape[1] // 4) if crossing is None else 0
    packed = pack(after(w_down, picked[0]), moment1, moment2, rows)
    waits = arrived[1:]
    states = []
    if rows:
        states.append(move(w_down[0, :rows]))
        waits = waits + states
    states.append(move(after(packed, *waits)))
    arrived[0] = after(arrived[0], packed)
    own_block, new_block = join_pieces(arrived)
    if crossing is None:
        new_half = gather_half(new_block)
        own_parts = gather_own(own_block, columns, new_half)
        factors = factors_of(own_parts, w_in, w_down, half, 1)
        new_parts = [new_half, crossed(after(new_half, *own_parts[:3]), lax.axis_size("dp") // 2)]
    else:
        own_parts = gather_own(own_block, columns, None)
        factors = factors_of(own_parts, w_in, w_down, half, 12)
        new_parts = gather_some(after(new_block, *own_parts[:3]), columns, crossing)
        pairs = [(order[s], s) for s in range(expert_count) if s not in crossing]
        new_parts.append(lax.ppermute(after(jnp.concatenate(own_parts, axis=0), factors), "expert", pairs))
    factors = move(factors)
    return tuple(finish(factors, crossing, new_parts, states, half, columns))


def local(tokens, grad_out, route_weights, expert_ids, swap_code, w_in, w_down, moment1, moment2):
    expert_count = lax.axis_size("expert")
    sections = expert_count.bit_length() - 1
    columns = max(1, expert_count // 2)
    operands = (tokens, grad_out, route_weights, expert_ids, w_in, w_down, moment1, moment2)

    free = [(b, s) for b in range(sections) for s in range(1, expert_count) if not s >> b & 1]
    fixed = [(b, 0) for b in range(sections)]
    if len(free) <= 2:
        branches = []
        for taken in itertools.product((False, True), repeat=len(free)):
            pairs = fixed + [pair for pair, yes in zip(free, taken) if yes]
            order = static_order(expert_count, sections, pairs)
            move = functools.partial(
                lax.ppermute, axis_name="expert", perm=[(order[s], s) for s in range(expert_count)]
            )
            branches.append(functools.partial(layer, move, columns, order))
        which = jnp.int32(0)
        for bit, slot in free:
            which = which * 2 + ((swap_code[slot] >> bit) & 1)
        return lax.switch(which, branches, operands)

    swaps = section_swaps(swap_code, lax.axis_index("expert"), sections)

    def move_by_sections(array):
        for bit in range(sections):
            pairs = [(i, i ^ (1 << bit)) for i in range(expert_count)]
            array = jnp.where(swaps[bit], lax.ppermute(array, "expert", pairs), array)
        return array

    slots = jnp.arange(expert_count, dtype=jnp.int32)
    order = slots
    for bit in range(sections):
        partner = jnp.bitwise_xor(slots, 1 << bit)
        swapped = swap_code[jnp.minimum(slots, partner)] // (1 << bit) % 2 == 1
        order = order[jnp.where(swapped, partner, slots)]
    return layer(move_by_sections, columns, [order[s] for s in range(expert_count)], operands)


def solution(mesh):
    placed = (
        P(("expert", "dp"), None),
        P(("expert", "dp"), None),
        P(("expert", "dp"), None),
        P(("expert", "dp"), None),
        P(),
        P("expert", None, "dp", None),
        P("expert", "dp", None),
        P("expert", "dp", None),
        P("expert", "dp", None),
    )
    return jax.shard_map(
        local,
        mesh=mesh,
        in_specs=placed,
        out_specs=(
            P("expert", "dp", None),
            P("expert", "dp", None),
            P("expert", "dp", None),
            P("expert", None, "dp", None),
        ),
        check_vma=False,
    )
```

```python
import functools
import itertools

import jax
import jax.numpy as jnp
from jax import lax
from jax.experimental import pallas as pl
from jax.experimental.pallas import tpu as pltpu
from jax.sharding import PartitionSpec as P

CAP = 5
PIECE = 24
VMEM_LIMIT = 60 * 1024 * 1024

adam_rate = 0.01
beta_one = 0.9
beta_two = 0.999
adam_step = 100.0
adam_eps = 1e-08


def dot(left_side, right_side, left_dim, right_dim):
    return lax.dot_general(
        left_side,
        right_side,
        (((left_dim,), (right_dim,)), ((), ())),
        preferred_element_type=jnp.float32,
    )


def params(limit=VMEM_LIMIT):
    return pltpu.CompilerParams(vmem_limit_bytes=limit)


def cost(flops, nbytes):
    return pl.CostEstimate(flops=int(flops), bytes_accessed=int(nbytes), transcendentals=0)


def tile_of(width, most):
    tile = 128
    for count in range(1, width // 128 + 1):
        if width % (count * 128) == 0 and count * 128 <= most:
            tile = count * 128
    return tile


def pick_kernel(order, pieces, *refs):
    if order is None:
        order, refs = [refs[0][s] for s in range(pieces)], refs[1:]
    ids_ref, weights_ref, tok_ref, grad_ref = refs[:4]
    outs, (sel, scale) = refs[4 : 4 + pieces], refs[4 + pieces :]
    rows = tok_ref.shape[0]
    own_slot = lax.axis_index("expert")

    @pl.when(pl.program_id(0) == 0)
    def _():
        ids = ids_ref[...]
        weights = weights_ref[...]
        earlier = (
            lax.broadcasted_iota(jnp.int32, (rows, rows), 0)
            < lax.broadcasted_iota(jnp.int32, (rows, rows), 1)
        ).astype(jnp.bfloat16)
        want_count = 2 * pieces
        place = lax.broadcasted_iota(jnp.int32, (want_count, rows), 0)
        hits = jnp.zeros((want_count, rows), jnp.float32)
        shares = []
        for piece in range(pieces):
            slot = jnp.bitwise_xor(own_slot, piece)
            source = jnp.int32(0)
            for target in range(pieces):
                source = jnp.where(slot == target, order[target], source)
            for role, expert in enumerate((slot, source)):
                named = ids == expert
                hit = jnp.max(jnp.where(named, 1.0, 0.0), axis=0, keepdims=True)
                hits = jnp.where(place == 2 * piece + role, hit, hits)
                shares.append(jnp.sum(jnp.where(named, weights, 0.0), axis=0, keepdims=True))
        ranks = dot(hits.astype(jnp.bfloat16), earlier, 1, 0)
        ranks = jnp.where(hits > 0.0, ranks, -1.0).astype(jnp.int32)
        row = lax.broadcasted_iota(jnp.int32, (PIECE, rows), 0)
        of_role = jnp.where(row >= 2 * CAP, row - 2 * CAP, row)
        is_grad = of_role >= CAP
        copy = jnp.where(is_grad, of_role - CAP, of_role)
        for piece in range(pieces):
            first, second = 2 * piece, 2 * piece + 1
            is_first = row < 2 * CAP
            rank = jnp.where(is_first, ranks[first : first + 1], ranks[second : second + 1])
            share = jnp.where(is_first, shares[first], shares[second])
            match = jnp.logical_and(copy == rank, row < 4 * CAP)
            part = pl.ds(piece * PIECE, PIECE)
            sel[0, part] = jnp.where(jnp.logical_and(match, jnp.logical_not(is_grad)), 1.0, 0.0)
            sel[1, part] = jnp.where(jnp.logical_and(match, is_grad), 1.0, 0.0)
            scale[part] = jnp.sum(jnp.where(match, share, 0.0), axis=1, keepdims=True)

    token_part = dot(sel[0].astype(jnp.bfloat16), tok_ref[...], 1, 0)
    grad_part = dot(sel[1].astype(jnp.bfloat16), grad_ref[...], 1, 0)
    picked = token_part + scale[...] * grad_part
    for piece in range(pieces):
        outs[piece][...] = picked[piece * PIECE : (piece + 1) * PIECE].astype(jnp.bfloat16)


def pick_rows(order, tokens, grad_out, route_weights, expert_ids):
    pieces = len(order)
    rows, width = tokens.shape
    top = expert_ids.shape[1]
    total = pieces * PIECE
    tile = tile_of(width, 1792)
    known = all(isinstance(s, int) for s in order)
    return pl.pallas_call(
        functools.partial(pick_kernel, tuple(order) if known else None, pieces),
        grid_spec=pltpu.PrefetchScalarGridSpec(
            num_scalar_prefetch=0 if known else 1,
            grid=(width // tile,),
            in_specs=[
                pl.BlockSpec((top, rows), lambda j, *_: (0, 0)),
                pl.BlockSpec((top, rows), lambda j, *_: (0, 0)),
                pl.BlockSpec((rows, tile), lambda j, *_: (0, j)),
                pl.BlockSpec((rows, tile), lambda j, *_: (0, j)),
            ],
            out_specs=[pl.BlockSpec((PIECE, tile), lambda j, *_: (0, j))] * pieces,
            scratch_shapes=[
                pltpu.VMEM((2, total, rows), jnp.float32),
                pltpu.VMEM((total, 1), jnp.float32),
            ],
        ),
        out_shape=[jax.ShapeDtypeStruct((PIECE, width), jnp.bfloat16)] * pieces,
        compiler_params=params(),
        cost_estimate=cost(4 * total * rows * width, 4 * rows * width),
        name="pick_rows",
    )(*(() if known else (jnp.stack(order),)), expert_ids.T, route_weights.T, tokens, grad_out)


def join_kernel(pieces, *refs):
    ins, (own_ref, new_ref) = refs[:pieces], refs[pieces:]
    half = pieces * CAP
    own_slot = lax.axis_index("expert")
    shape = (4 * half, pieces * PIECE)
    row = lax.broadcasted_iota(jnp.int32, shape, 0)
    column = lax.broadcasted_iota(jnp.int32, shape, 1)
    is_second = row >= 2 * half
    of_role = jnp.where(is_second, row - 2 * half, row)
    is_grad = of_role >= half
    in_half = jnp.where(is_grad, of_role - half, of_role)
    chosen = jnp.zeros(shape, jnp.float32)
    for mask in range(pieces):
        copy = in_half - jnp.bitwise_xor(own_slot, mask) * CAP
        wanted = copy + jnp.where(is_grad, CAP, 0) + jnp.where(is_second, 2 * CAP, 0) + mask * PIECE
        mine = jnp.logical_and(copy >= 0, copy < CAP)
        chosen = chosen + jnp.where(jnp.logical_and(mine, column == wanted), 1.0, 0.0)
    rows = jnp.concatenate([ref[...] for ref in ins], axis=0)
    both = dot(chosen.astype(jnp.bfloat16), rows, 1, 0)
    own_ref[...] = both[: 2 * half].astype(jnp.bfloat16)
    new_ref[...] = both[2 * half :].astype(jnp.bfloat16)


def join_pieces(arrays):
    pieces, width = len(arrays), arrays[0].shape[1]
    total = 2 * pieces * CAP
    tile = tile_of(width, 1792)
    return pl.pallas_call(
        functools.partial(join_kernel, pieces),
        grid=(width // tile,),
        in_specs=[pl.BlockSpec((PIECE, tile), lambda j: (0, j))] * pieces,
        out_specs=[pl.BlockSpec((total, tile), lambda j: (0, j))] * 2,
        out_shape=[jax.ShapeDtypeStruct((total, width), jnp.bfloat16)] * 2,
        compiler_params=params(VMEM_LIMIT // 2),
        cost_estimate=cost(4 * total * PIECE * pieces * width, 8 * total * width),
        name="join_pieces",
    )(*arrays)


def rows_apart(refs, half, columns=None):
    blocks = [(ref, first) for ref in refs for first in range(0, ref.shape[0], 2 * half)]
    if columns is not None:
        blocks = [block for column in range(columns) for block in blocks[column::columns]]
    token_rows = jnp.concatenate([ref[first : first + half] for ref, first in blocks], axis=0)
    grad_rows = jnp.concatenate([ref[first + half : first + 2 * half] for ref, first in blocks], axis=0)
    return token_rows, grad_rows


def parts_spec(parts, tile):
    return [pl.BlockSpec((part.shape[0], tile), lambda j: (0, j)) for part in parts]


def factor_kernel(half, *refs):
    (w_in_ref, w_down_ref, out_ref, acc), x_refs = refs[-4:], refs[:-4]
    step = pl.program_id(0)
    units = w_down_ref.shape[1]

    @pl.when(step == 0)
    def _():
        acc[...] = jnp.zeros_like(acc)

    token_rows, grad_rows = rows_apart(x_refs, half)
    acc[0] += dot(token_rows, w_in_ref[0, 0], 1, 1)
    acc[1] += dot(token_rows, w_in_ref[0, 1], 1, 1)
    acc[2] += dot(grad_rows, w_down_ref[0], 1, 1)

    @pl.when(step == pl.num_programs(0) - 1)
    def _():
        gate, up, back = acc[0], acc[1], acc[2]
        sig = jax.nn.sigmoid(gate)
        activated = gate * sig
        slopes = sig * (1.0 + gate * (1.0 - sig))
        out_ref[:, 0:units] = (back * up * slopes).astype(jnp.bfloat16)
        out_ref[:, units : 2 * units] = (back * activated).astype(jnp.bfloat16)
        out_ref[:, 2 * units : 3 * units] = (activated * up).astype(jnp.bfloat16)


def factors_of(parts, w_in, w_down, half, weight):
    count, width = sum(part.shape[0] for part in parts) // 2, parts[0].shape[1]
    units = w_down.shape[1]
    tile = tile_of(width, 896)
    return pl.pallas_call(
        functools.partial(factor_kernel, half),
        grid=(width // tile,),
        in_specs=[
            *parts_spec(parts, tile),
            pl.BlockSpec((1, 2, units, tile), lambda j: (0, 0, 0, j)),
            pl.BlockSpec((1, units, tile), lambda j: (0, 0, j)),
        ],
        out_specs=pl.BlockSpec((count, 3 * units), lambda j: (0, 0)),
        out_shape=jax.ShapeDtypeStruct((count, 3 * units), jnp.bfloat16),
        scratch_shapes=[pltpu.VMEM((3, count, units), jnp.float32)],
        compiler_params=params(VMEM_LIMIT // 2),
        cost_estimate=cost(6 * weight * count * units * width, 6 * units * width + 4 * count * width),
        name="factors",
    )(*parts, w_in, w_down)


def pack_kernel(first, w_ref, one_ref, two_ref, out_ref):
    units = one_ref.shape[1]
    out_ref[: units - first] = w_ref[0, first:]
    out_ref[units - first : 2 * units - first] = one_ref[0].astype(jnp.bfloat16)
    out_ref[2 * units - first :] = two_ref[0].astype(jnp.bfloat16)


def pack(w_down, moment1, moment2, first):
    _, units, width = w_down.shape
    tile = tile_of(width, 896)
    spec = pl.BlockSpec((1, units, tile), lambda j: (0, 0, j))
    return pl.pallas_call(
        functools.partial(pack_kernel, first),
        grid=(width // tile,),
        in_specs=[spec, spec, spec],
        out_specs=pl.BlockSpec((3 * units - first, tile), lambda j: (0, j)),
        out_shape=jax.ShapeDtypeStruct((3 * units - first, width), jnp.bfloat16),
        compiler_params=params(),
        cost_estimate=cost(2 * units * width, 16 * units * width),
        name="pack_state",
    )(w_down, moment1, moment2)


def finish_kernel(half, columns, crossing, count, factor_ref, *refs):
    (down_ref, one_ref, two_ref, grad_ref, turned), x_refs = refs[-5:], refs[count:-5]
    units = down_ref.shape[1]

    @pl.when(pl.program_id(0) == 0)
    def _():
        turned[...] = factor_ref[...].astype(jnp.float32).T.astype(jnp.bfloat16)

    if crossing is None:
        token_rows, grad_rows = rows_apart(x_refs, half, columns)
    else:
        own_slot = lax.axis_index("expert")
        gathered = functools.reduce(jnp.logical_or, [own_slot == slot for slot in crossing])
        pairs = zip(rows_apart(x_refs[:-1], half), rows_apart(x_refs[-1:], half))
        token_rows, grad_rows = [jnp.where(gathered, theirs, mine) for theirs, mine in pairs]
    in_grads = dot(turned[: 2 * units], token_rows, 1, 0).astype(jnp.bfloat16)
    grad_ref[0, 0] = in_grads[:units]
    grad_ref[0, 1] = in_grads[units:]
    down_grad = dot(turned[2 * units :], grad_rows, 1, 0)
    rest = refs[count - 1]
    split = rest.shape[0] - 2 * units
    w_down = [refs[0][...], rest[:split]] if count == 2 else [rest[:split]]
    w_down = jnp.concatenate([part.astype(jnp.float32) for part in w_down], axis=0)
    moment1 = rest[split : split + units].astype(jnp.float32)
    moment2 = rest[split + units :].astype(jnp.float32)
    rate = adam_rate / (1.0 - beta_one**adam_step)
    fix_two = 1.0 / (1.0 - beta_two**adam_step)
    first_new = beta_one * moment1 + (1.0 - beta_one) * down_grad
    second_new = beta_two * moment2 + (1.0 - beta_two) * (down_grad * down_grad)
    change = rate * first_new / (jnp.sqrt(second_new * fix_two) + adam_eps)
    down_ref[0] = (w_down - change).astype(jnp.bfloat16)
    one_ref[0] = first_new
    two_ref[0] = second_new


def finish(factors, crossing, parts, states, half, columns):
    count, width = factors.shape[0], parts[0].shape[1]
    units = factors.shape[1] // 3
    tile = tile_of(width, 896)
    spec = pl.BlockSpec((1, units, tile), lambda j: (0, 0, j))
    kinds = (jnp.bfloat16, jnp.float32, jnp.float32)
    return pl.pallas_call(
        functools.partial(finish_kernel, half, columns, crossing, len(states)),
        grid=(width // tile,),
        in_specs=[
            pl.BlockSpec((count, 3 * units), lambda j: (0, 0)),
            *parts_spec(states, tile),
            *parts_spec(parts, tile),
        ],
        out_specs=[spec, spec, spec, pl.BlockSpec((1, 2, units, tile), lambda j: (0, 0, 0, j))],
        out_shape=[jax.ShapeDtypeStruct((1, units, width), kind) for kind in kinds]
        + [jax.ShapeDtypeStruct((1, 2, units, width), jnp.bfloat16)],
        scratch_shapes=[pltpu.VMEM((3 * units, count), jnp.bfloat16)],
        compiler_params=params(VMEM_LIMIT // 2),
        cost_estimate=cost(6 * count * units * width, 20 * units * width + 4 * count * width),
        name="finish",
    )(factors, *states, *parts)


def crossed(array, mask, slots=None):
    size = lax.axis_size("dp")
    if slots is None:
        return lax.ppermute(array, "dp", [(i, i ^ mask) for i in range(size)])
    pairs = [(s * size + i, s * size + (i ^ mask)) for s in slots for i in range(size)]
    return lax.ppermute(array, ("expert", "dp"), pairs)


def gather_own(block, columns, wait):
    planes = lax.axis_size("dp") // columns
    blocks = [block, crossed(block, columns)]
    for k in range(2, planes):
        blocks.append(crossed(block if k % 2 else after(block, blocks[1]), k * columns))
    near = jnp.concatenate(blocks[: planes // 2], axis=0)
    far = jnp.concatenate(blocks[planes // 2 :], axis=0)
    far = far if wait is None else after(far, wait)
    return [near, far] + [crossed(part, k) for k in range(1, columns) for part in (near, far)]


def gather_some(block, columns, slots):
    planes = lax.axis_size("dp") // columns
    blocks = [crossed(block, k * columns, slots) for k in reversed(range(1, planes))]
    blocks = [block] + blocks[::-1]
    near = jnp.concatenate(blocks[: planes // 2], axis=0)
    far = jnp.concatenate(blocks[planes // 2 :], axis=0)
    return [near, far] + [crossed(part, k, slots) for k in range(1, columns) for part in (near, far)]


def gather_half(block):
    held, mask = block, 1
    while 2 * mask < lax.axis_size("dp"):
        held = jnp.concatenate([held, crossed(held, mask)], axis=0)
        mask = 2 * mask
    return held


def after(array, *others):
    return lax.optimization_barrier((array, *others))[0]


def section_swaps(swap_code, slot, sections):
    swaps = []
    for bit in range(sections):
        lower = jnp.minimum(slot, jnp.bitwise_xor(slot, 1 << bit))
        swaps.append(swap_code[lower] // (1 << bit) % 2 == 1)
    return swaps


def static_order(expert_count, sections, swapped_pairs):
    order = list(range(expert_count))
    for bit in range(sections):
        step = [s ^ (1 << bit) if (bit, min(s, s ^ (1 << bit))) in swapped_pairs else s for s in range(expert_count)]
        order = [order[s] for s in step]
    return order


def layer(move, columns, order, operands):
    tokens, grad_out, route_weights, expert_ids, w_in, w_down, moment1, moment2 = operands
    expert_count = len(order)
    half = expert_count * CAP
    crossing = None
    if all(isinstance(slot, int) for slot in order):
        crossing = [s for s in range(expert_count) if order[s] not in (s, s ^ 1)]
    if crossing is not None and len(crossing) == expert_count:
        crossing = None

    picked = pick_rows(order, tokens, grad_out, route_weights, expert_ids)
    arrived = [picked[0]]
    for mask in range(1, expert_count):
        pairs = [(i, i ^ mask) for i in range(expert_count)]
        arrived.append(lax.ppermute(picked[mask], "expert", pairs))
    rows = max(16, w_down.shape[1] // 4) if crossing is None else 0
    packed = pack(after(w_down, picked[0]), moment1, moment2, rows)
    waits = arrived[1:]
    states = []
    if rows:
        states.append(move(w_down[0, :rows]))
        waits = waits + states
    states.append(move(after(packed, *waits)))
    arrived[0] = after(arrived[0], packed)
    own_block, new_block = join_pieces(arrived)
    if crossing is None:
        new_half = gather_half(new_block)
        own_parts = gather_own(own_block, columns, new_half)
        factors = factors_of(own_parts, w_in, w_down, half, 1)
        new_parts = [new_half, crossed(after(new_half, *own_parts[:3]), lax.axis_size("dp") // 2)]
    else:
        own_parts = gather_own(own_block, columns, None)
        factors = factors_of(own_parts, w_in, w_down, half, 12)
        new_parts = gather_some(after(new_block, *own_parts[:3]), columns, crossing)
        pairs = [(order[s], s) for s in range(expert_count) if s not in crossing]
        new_parts.append(lax.ppermute(after(jnp.concatenate(own_parts, axis=0), factors), "expert", pairs))
    factors = move(factors)
    return tuple(finish(factors, crossing, new_parts, states, half, columns))


def local(tokens, grad_out, route_weights, expert_ids, swap_code, w_in, w_down, moment1, moment2):
    expert_count = lax.axis_size("expert")
    sections = expert_count.bit_length() - 1
    columns = max(1, expert_count // 2)
    operands = (tokens, grad_out, route_weights, expert_ids, w_in, w_down, moment1, moment2)

    free = [(b, s) for b in range(sections) for s in range(1, expert_count) if not s >> b & 1]
    fixed = [(b, 0) for b in range(sections)]
    if len(free) <= 2:
        branches = []
        for taken in itertools.product((False, True), repeat=len(free)):
            pairs = fixed + [pair for pair, yes in zip(free, taken) if yes]
            order = static_order(expert_count, sections, pairs)
            move = functools.partial(
                lax.ppermute, axis_name="expert", perm=[(order[s], s) for s in range(expert_count)]
            )
            branches.append(functools.partial(layer, move, columns, order))
        which = jnp.int32(0)
        for bit, slot in free:
            which = which * 2 + ((swap_code[slot] >> bit) & 1)
        return lax.switch(which, branches, operands)

    swaps = section_swaps(swap_code, lax.axis_index("expert"), sections)

    def move_by_sections(array):
        for bit in range(sections):
            pairs = [(i, i ^ (1 << bit)) for i in range(expert_count)]
            array = jnp.where(swaps[bit], lax.ppermute(array, "expert", pairs), array)
        return array

    slots = jnp.arange(expert_count, dtype=jnp.int32)
    order = slots
    for bit in range(sections):
        partner = jnp.bitwise_xor(slots, 1 << bit)
        swapped = swap_code[jnp.minimum(slots, partner)] // (1 << bit) % 2 == 1
        order = order[jnp.where(swapped, partner, slots)]
    return layer(move_by_sections, columns, [order[s] for s in range(expert_count)], operands)


def solution(mesh):
    placed = (
        P(("expert", "dp"), None),
        P(("expert", "dp"), None),
        P(("expert", "dp"), None),
        P(("expert", "dp"), None),
        P(),
        P("expert", None, "dp", None),
        P("expert", "dp", None),
        P("expert", "dp", None),
        P("expert", "dp", None),
    )
    return jax.shard_map(
        local,
        mesh=mesh,
        in_specs=placed,
        out_specs=(
            P("expert", "dp", None),
            P("expert", "dp", None),
            P("expert", "dp", None),
            P("expert", None, "dp", None),
        ),
        check_vma=False,
    )
```
